128 devices in a mesh: slab: 16 (over z, x), helper: 8 (over y, core).
Axes of the slice: x: 4, y: 4, z: 4, core: 2. Of those that a mesh axis runs over, the one named last changes fastest.
Arguments:
- disp: float32 [400, 3, 16384], P(None, None, ('slab', 'helper')), may hold values from -2 to 2
- strain: float32 [9, 16384], P(None, ('slab', 'helper')), may hold values from -6 to 6
- counts: int32 [16384], P(('slab', 'helper')), may hold values from 3 to 12
- assign: int32 [16384, 1], P(('slab', 'helper')), may hold values from 0 to 127; in each aligned block of 128 rows (0 to 127, 128 to 255, ...) at most 2 rows name the same one
- cached_pos: float32 [400, 3, 32768], P(None, None, ('slab', 'helper')), may hold values from -1 to 1
- contact_mask: int32 [400, 400], replicated, may hold values from 0 to 1, as said below
- node_index: int32 [8, 16384], P(None, ('slab', 'helper')), may hold values from 0 to 4095, as said below
- node_grads: float32 [3, 8, 16384], P(None, None, ('slab', 'helper')), may hold values from -6 to 6
Outputs:
- disp_out: float32 [400, 3, 16384], P(None, None, ('slab', 'helper'))
- stress: float32 [9, 16384], P(None, ('slab', 'helper'))
- grid_force: float32 [3, 32, 1024], P(None, 'slab', 'helper')
The draws below stay inside these ranges and needn't reach their ends.
Inputs may be any that keep to these rules, and one draw needn't show every extreme that they name: `contact_mask`: symmetric 0/1 matrix with zero diagonal. `node_index`: each point's eight values are the corners of one cell: layers l and l + 1 with l from 0 to 2, rows i and i + 1, columns j and j + 1 of a 32 x 32 layer, value layer * 1024 + row * 32 + column. `assign`: within one device's 128 points no helper is named more than 2 times. `cached_pos`: column d * 128 * 2 + s * 2 + c holds the packing of the c-th point, in order, among the points of block s that name helper d; other columns are not used.
All inputs are finite; a program needn't handle non-finite values.
Results may differ from the reference program's by a relative error of at most 0.0003.
Values sent between devices are 32-bit elements; how exact they have to be, the bound alone decides.
A program may use at most 64 MiB of HBM per device.

```python
import math
import jax
import jax.numpy as jnp
import numpy as np
from jax import lax

GRAINS = 400
CONTACTS = 6
IT_LO = 3
IT_HI = 12
PTS_DEV = 128
LAYERS = 2
PSIDE = 32
PLANE = 1024
NPTS = 16384
CAP = 2
NLAYERS = 32
N_SLAB = 16
N_HELPER = 8
DEVICES = 128


def draw_counts(key, part):
    key = jax.random.fold_in(key, 11)
    k_band, k_low, k_high, k_top, k_bottom = jax.random.split(key, 5)
    middle = IT_HI // 2 + 1
    band = jax.random.randint(k_band, (NPTS,), 0, 8) == 0
    low = jax.random.randint(k_low, (NPTS,), IT_LO, middle)
    high = jax.random.randint(k_high, (NPTS,), middle, IT_HI + 1)
    values = jnp.where(band, high, low)
    top_at = jax.random.randint(k_top, (), 0, NPTS // 2)
    bottom_at = jax.random.randint(k_bottom, (), NPTS // 2, NPTS)
    values = values.at[top_at].set(IT_HI).at[bottom_at].set(IT_LO)
    return values.astype(jnp.int32)


def draw_contact_mask(key, part):
    key = jax.random.fold_in(key, 23)
    picks = jax.random.randint(key, (GRAINS, GRAINS), 0, GRAINS) < CONTACTS
    rows = jnp.arange(GRAINS)[:, None]
    cols = jnp.arange(GRAINS)[None, :]
    upper = picks & (cols > rows)
    return (upper | upper.T).astype(jnp.int32)


def draw_node_index(key, part):
    key = jax.random.fold_in(key, 37)
    k_layer, k_row, k_col, k_top, k_bottom = jax.random.split(key, 5)
    base = jax.random.randint(k_layer, (NPTS,), 0, LAYERS + 1)
    row = jax.random.randint(k_row, (NPTS,), 0, PSIDE - 1)
    col = jax.random.randint(k_col, (NPTS,), 0, PSIDE - 1)
    top_at = jax.random.randint(k_top, (), 0, NPTS // 2)
    bottom_at = jax.random.randint(k_bottom, (), NPTS // 2, NPTS)
    base = base.at[top_at].set(LAYERS).at[bottom_at].set(0)
    row = row.at[top_at].set(PSIDE - 2).at[bottom_at].set(0)
    col = col.at[top_at].set(PSIDE - 2).at[bottom_at].set(0)
    layer_step = jnp.array([0, 0, 0, 0, 1, 1, 1, 1], jnp.int32)[:, None]
    row_step = jnp.array([0, 0, 1, 1, 0, 0, 1, 1], jnp.int32)[:, None]
    col_step = jnp.array([0, 1, 0, 1, 0, 1, 0, 1], jnp.int32)[:, None]
    values = (base[None, :] + layer_step) * PLANE + (row[None, :] + row_step) * PSIDE + col[None, :] + col_step
    return values.astype(jnp.int32)


def levels(rng, dims, pieces, smallest, high):
    def one(axis_at, shards_of):
        draws = jax.random.uniform(jax.random.fold_in(jax.random.fold_in(rng, 6), axis_at), (shards_of,), jnp.float32, smallest / len(pieces), high / len(pieces))
        return jnp.repeat(jnp.exp(draws), dims[axis_at] // shards_of).reshape((-1,) + (1,) * (len(dims) - axis_at - 1))

    factor_of = one(*pieces[0])
    for cut in pieces[1:]:
        factor_of = factor_of * one(*cut)
    return factor_of


def assign_block(stream_key, own, number, rows, amount, top, bound, lean):
    order = jax.random.permutation(stream_key, amount)
    heavy_load, usual = load_shares(amount, rows * top, bound, lean, True), load_shares(amount, rows * top, bound, lean, False)
    places = jnp.arange(amount)

    def named(tallies, offset_by):
        used = int((tallies > 0).sum())
        fixed = max(1, used // 4)
        shifted = fixed + (places - fixed + offset_by * (used - fixed)) % max(1, amount - fixed)
        return jnp.zeros((amount,), jnp.int32).at[order[jnp.where(places < fixed, places, shifted)]].set(jnp.asarray(tallies, jnp.int32))

    tallies = jnp.where(number % 4 == 0, named(heavy_load, number // 4), named(usual, number - number // 4 - 1))
    mixed = jax.random.permutation(jax.random.fold_in(own, 3), amount)
    giver, taker = mixed[0:amount // 2 * 2:2], mixed[1:amount // 2 * 2:2]
    room = jnp.minimum(tallies[giver] - 1, bound - tallies[taker]) // 2
    room = jnp.where((giver == order[0]) | (taker == order[0]) | (tallies[taker] == 0), 0, jnp.maximum(room, 0))
    shifted = jax.random.randint(jax.random.fold_in(own, 4), (amount // 2,), 0, 1 << 20) % (room + 1)
    tallies = tallies.at[giver].add(-shifted).at[taker].add(shifted)
    members = jnp.searchsorted(jnp.cumsum(tallies), jnp.arange(rows * top), side="right").astype(jnp.int32)
    table = members.reshape(top, rows).T
    table = table[jax.random.permutation(jax.random.fold_in(own, 1), rows)]
    offset_by = jax.random.randint(jax.random.fold_in(own, 2), (rows, 1), 0, top)
    return jnp.take_along_axis(table, (jnp.arange(top)[None, :] + offset_by) % top, axis=1)


def load_shares(count, total, most, slope, full):
    weights = [(1 << 20) // math.isqrt(grade ** slope) + 1 for grade in range(1, count + 1)]
    largest = most if full else min(most, max(-(-total // count), total * weights[0] // sum(weights)))
    least = 1 if total - largest >= count - 1 else 0
    holding, rest = [largest] + [least] * (count - 1), total - largest - least * (count - 1)
    while rest > 0:
        free = [i for i in range(1, count) if holding[i] < largest] or [i for i in range(1, count) if holding[i] < most]
        whole, left = sum([weights[i] for i in free]), rest
        for i in free:
            more = min(most - holding[i], max(1, left * weights[i] // whole), rest)
            holding[i] = holding[i] + more
            rest = rest - more
    return np.array(holding)


def centred(stream_key, dims, spread, most, cuts=(), kind=jnp.bfloat16):
    factor_of = levels(stream_key, dims, cuts, -0.22, 0.18) if cuts else 1.0
    entries = jax.random.normal(stream_key, dims, jnp.float32) * spread * factor_of
    return jnp.minimum(jnp.maximum(entries, -most), most).astype(kind)


def setup_inputs(seed: int = 0) -> dict:
    key_list = jax.random.split(jax.random.key(seed), 9)
    disp = centred(key_list[0], (GRAINS, 3, NPTS), 0.3, 2.0, ((2, 128),), jnp.float32)
    strain = centred(key_list[1], (9, NPTS), 1.0, 6.0, ((1, 128),), jnp.float32)
    counts = draw_counts(jax.random.fold_in(key_list[8], 71), 0)
    assign_keys = jax.random.split(jax.random.fold_in(key_list[3], 1), NPTS // PTS_DEV)
    assign_turns = jax.random.permutation(jax.random.fold_in(key_list[3], 3), NPTS // PTS_DEV)
    assign = jax.vmap(lambda own, number: assign_block(jax.random.fold_in(key_list[3], 2), own, number, PTS_DEV, DEVICES, 1, CAP, 2))(assign_keys, assign_turns).reshape((NPTS, 1))
    cached_pos = jnp.clip(jax.random.uniform(key_list[4], (GRAINS, 3, DEVICES * DEVICES * CAP), jnp.float32, -1.0, 1.0) * levels(key_list[4], (GRAINS, 3, DEVICES * DEVICES * CAP), ((2, 128),), -0.4, 0.0), -1.0, 1.0)
    contact_mask = draw_contact_mask(jax.random.fold_in(key_list[8], 71), 0)
    node_index = draw_node_index(jax.random.fold_in(key_list[8], 71), 0)
    node_grads = centred(key_list[7], (3, 8, NPTS), 1.0, 6.0, ((2, 128),), jnp.float32)
    return dict(disp=disp, strain=strain, counts=counts, assign=assign, cached_pos=cached_pos, contact_mask=contact_mask, node_index=node_index, node_grads=node_grads)


OMEGA = 0.8
GROUND = 1.0
HIGHEST = lax.Precision.HIGHEST


def reference(disp, strain, counts, assign, cached_pos, contact_mask, node_index, node_grads):
    devices = N_SLAB * N_HELPER
    target = assign[:, 0].reshape(devices, PTS_DEV)
    order = jnp.arange(PTS_DEV, dtype=jnp.int32)

    def ranking(row):
        same = row[:, None] == row[None, :]
        earlier = order[None, :] < order[:, None]
        return jnp.sum((same & earlier).astype(jnp.int32), axis=1).astype(jnp.int32)

    position = lax.map(ranking, target)
    source = jnp.arange(devices, dtype=jnp.int32)[:, None]
    column = (target * (devices * CAP) + source * CAP + position).reshape(-1).astype(jnp.int32)
    pos = jnp.take(cached_pos, column, axis=2)
    stiff = contact_mask.astype(jnp.float32)
    scale = (jnp.sum(stiff, axis=1) + GROUND)[:, None, None]
    strain_mat = strain.reshape(3, 3, -1)
    loading = jnp.einsum('dep,gep->gdp', strain_mat, pos, precision=HIGHEST)
    current = disp
    for sweep_index in range(IT_HI):
        mixed = jnp.dot(stiff, current.reshape(GRAINS, -1), precision=HIGHEST).reshape(current.shape)
        updated = current + OMEGA * (loading - scale * current + mixed) / scale
        current = jnp.where(sweep_index < counts, updated, current)
    mixed = jnp.dot(stiff, current.reshape(GRAINS, -1), precision=HIGHEST).reshape(current.shape)
    internal = scale * current - mixed
    moments = jnp.einsum('gdp,gep->dep', internal, pos, precision=HIGHEST) / GRAINS
    sigma = 0.5 * (moments + jnp.transpose(moments, (1, 0, 2)))
    contrib = jnp.einsum('cdp,dkp->ckp', -sigma, node_grads, precision=HIGHEST)
    slab_of = (jnp.arange(NPTS, dtype=jnp.int32) // (PTS_DEV * N_HELPER)).astype(jnp.int32)
    layer_of = node_index // PLANE
    within = node_index % PLANE
    global_layer = slab_of[None, :] * LAYERS + layer_of - 1
    valid = (global_layer >= 0) & (global_layer < NLAYERS)
    target_node = jnp.where(valid, global_layer * PLANE + within, NLAYERS * PLANE).astype(jnp.int32)
    grid = jnp.zeros((3, NLAYERS * PLANE + 1), jnp.float32).at[:, target_node.reshape(-1)].add(contrib.reshape(3, -1))
    grid_force = grid[:, :-1].reshape(3, NLAYERS, PLANE)
    return current, sigma.reshape(9, -1), grid_force
```

```python
import jax
import jax.numpy as jnp
from jax import lax
from jax.experimental import pallas as pl
from jax.experimental.pallas import tpu as pltpu
from jax.sharding import PartitionSpec as P

MESH = pl.DeviceIdType.MESH
GRAINS = 400
FLAT = 1200
POINTS = 128
SLOTS = 256
HELPERS = 8
SLABS = 16
DEVICES = 128
CHUNKS = 10
ROWS = 2 * CHUNKS
IT_HI = 12
F32 = jnp.float32
BF16 = jnp.bfloat16


def halves(x):
    hi = x.astype(BF16)
    lo = (x - hi.astype(F32)).astype(BF16)
    return hi, lo


def dot(a, b):
    return jnp.dot(a, b, preferred_element_type=F32)


def dot_nt(a, b):
    return lax.dot_general(a, b, (((1,), (1,)), ((), ())), preferred_element_type=F32)


def mixed(stiff, x):
    hi, lo = halves(x)
    return dot(stiff, hi) + dot(stiff, lo)


def at_device(index):
    return (index // HELPERS, lax.rem(index, HELPERS))


def kernel(
    cached_hbm, disp_hbm, mask_ref, strain_ref, counts_ref, assign_ref, node_ref, grads_ref,
    disp_out_hbm, stress_ref, grid_ref,
    cached, sent, got, part, sum_part, pos, stiff_ref, rate_ref, force,
    grid_out, own_got, low_got, high_got,
    load_sem, send_sem, recv_sem, own_sem, out_sem, grid_send, grid_recv,
):
    slab = lax.axis_index("slab")
    helper = lax.axis_index("helper")
    me = slab * HELPERS + helper

    load_cached = pltpu.make_async_copy(cached_hbm, cached, load_sem.at[0])
    load_cached.start()
    loads = []
    for d in range(3):
        copy = pltpu.make_async_copy(
            disp_hbm.at[pl.ds(d * GRAINS, GRAINS)],
            part.at[:, pl.ds(d * POINTS, POINTS)],
            load_sem.at[1 + d],
        )
        copy.start()
        loads.append(copy)

    barrier = pltpu.get_barrier_semaphore()

    def greet(step, carry):
        other = lax.rem(me + step, DEVICES)
        pl.semaphore_signal(barrier, inc=1, device_id=at_device(other), device_id_type=MESH)
        return carry

    lax.fori_loop(1, DEVICES, greet, 0)

    load_cached.wait()
    for k in range(CHUNKS):
        rows = min(128, FLAT - 128 * k)
        tile = cached[pl.ds(128 * k, rows), :]
        if rows < 128:
            tile = jnp.concatenate([tile, jnp.zeros((128 - rows, SLOTS), F32)], axis=0)
        sent[pl.ds(k, SLOTS, stride=CHUNKS), :] = tile.T

    pl.semaphore_wait(barrier, DEVICES - 1)

    def send(step, carry):
        other = lax.rem(me + step, DEVICES)
        pltpu.make_async_remote_copy(
            src_ref=sent.at[pl.ds(other * ROWS, ROWS)],
            dst_ref=got.at[pl.ds(me * ROWS, ROWS)],
            send_sem=send_sem,
            recv_sem=recv_sem,
            device_id=at_device(other),
            device_id_type=MESH,
        ).start()
        return carry

    lax.fori_loop(1, DEVICES, send, 0)
    own = pltpu.make_async_copy(
        sent.at[pl.ds(me * ROWS, ROWS)], got.at[pl.ds(me * ROWS, ROWS)], own_sem
    )
    own.start()

    stiff = mask_ref[...].astype(F32)
    scale = jnp.sum(stiff, axis=1, keepdims=True) + 1.0
    stiff_ref[...] = stiff.astype(BF16)
    rate_ref[...] = jnp.broadcast_to(0.8 / scale, (GRAINS, POINTS))
    counts = jnp.concatenate([counts_ref[...]] * 3, axis=1)

    def rate3():
        return jnp.concatenate([rate_ref[...]] * 3, axis=1)

    for copy in loads:
        copy.wait()

    def first(sweep, carry):
        u = part[...]
        new = 0.2 * u + rate3() * mixed(stiff_ref[...], u)
        part[...] = jnp.where(sweep < counts, new, u)
        return carry

    lax.fori_loop(0, IT_HI, first, 0)

    a_row = jnp.broadcast_to(assign_ref[...], (POINTS, POINTS))
    a_col = a_row.T
    p_at = lax.broadcasted_iota(jnp.int32, (POINTS, POINTS), 0)
    q_at = lax.broadcasted_iota(jnp.int32, (POINTS, POINTS), 1)
    rank = jnp.sum(
        jnp.where((a_row == a_col) & (q_at < p_at), 1.0, 0.0), axis=1, keepdims=True
    ).astype(jnp.int32)
    column = a_col * 2 + rank
    column = jnp.concatenate([column, column], axis=1)
    slot_at = lax.broadcasted_iota(jnp.int32, (POINTS, SLOTS), 1)
    pick = jnp.where(column == slot_at, 1.0, 0.0).astype(BF16)

    everything = sent.at[pl.ds(0, (DEVICES - 1) * ROWS)]
    own.wait()
    pltpu.make_async_copy(everything, everything, recv_sem).wait()

    for k in range(CHUNKS):
        hi, lo = halves(got[pl.ds(k, SLOTS, stride=CHUNKS), :])
        pos[pl.ds(128 * k, 128), :] = (dot(pick, hi) + dot(pick, lo)).T

    def position(e):
        return pos[pl.ds(e * GRAINS, GRAINS), :]

    for d in range(3):
        loading = sum(strain_ref[pl.ds(3 * d + e, 1), :] * position(e) for e in range(3))
        sum_part[:, pl.ds(d * POINTS, POINTS)] = rate_ref[...] * loading
    force[...] = sum_part[...]

    def second(sweep, carry):
        u = sum_part[...]
        new = 0.2 * u + rate3() * mixed(stiff_ref[...], u) + force[...]
        sum_part[...] = jnp.where(sweep < counts, new, u)
        return carry

    lax.fori_loop(1, IT_HI, second, 0)

    relaxed = part[...] + sum_part[...]
    part[...] = relaxed
    stores = []
    for d in range(3):
        copy = pltpu.make_async_copy(
            part.at[:, pl.ds(d * POINTS, POINTS)],
            disp_out_hbm.at[pl.ds(d * GRAINS, GRAINS)],
            out_sem.at[d],
        )
        copy.start()
        stores.append(copy)
    scale3 = 0.8 / rate3()
    internal = scale3 * relaxed - mixed(stiff_ref[...], relaxed)
    moments = [
        [
            jnp.sum(internal[:, d * POINTS : (d + 1) * POINTS] * position(e), axis=0, keepdims=True)
            / GRAINS
            for e in range(3)
        ]
        for d in range(3)
    ]
    stress = [[0.5 * (moments[d][e] + moments[e][d]) for e in range(3)] for d in range(3)]
    for d in range(3):
        for e in range(3):
            stress_ref[pl.ds(3 * d + e, 1), :] = stress[d][e]

    contrib = [-sum(stress[c][d] * grads_ref[d] for d in range(3)) for c in range(3)]
    row_at = lax.broadcasted_iota(jnp.int32, (128, POINTS), 0)
    total = jnp.zeros((128, 128), F32)
    for k in range(8):
        node = node_ref[pl.ds(k, 1), :]
        layer = node // 1024
        target = lax.rem(node, 1024) // 128
        low = lax.rem(node, 128)
        spread = jnp.where(row_at == low, 1.0, 0.0).astype(BF16)
        value = jnp.zeros((128, POINTS), F32)
        for c in range(3):
            value = jnp.where(row_at == target * 16 + layer * 4 + c, contrib[c][k : k + 1, :], value)
        hi, rest = halves(value)
        mid, low_part = halves(value - hi.astype(F32))
        total = total + dot_nt(hi, spread) + dot_nt(mid, spread) + dot_nt(low_part, spread)
    grid_out[...] = total
    below = lax.rem(slab + SLABS - 1, SLABS)
    above = lax.rem(slab + 1, SLABS)

    def grid_copy(first_row, count, kind, buffer, to_slab, to_helper):
        return pltpu.make_async_remote_copy(
            src_ref=grid_out.at[pl.ds(to_helper * 16 + first_row, count)],
            dst_ref=buffer.at[helper],
            send_sem=grid_send.at[kind],
            recv_sem=grid_recv.at[kind],
            device_id=(to_slab, to_helper),
            device_id_type=MESH,
        )

    def grid_sends(step, carry):
        to = lax.rem(helper + step, HELPERS)
        grid_copy(4, 8, 0, own_got, slab, to).start()
        return carry

    def grid_ghosts(step, carry):
        to = lax.rem(helper + step, HELPERS)
        grid_copy(0, 4, 1, high_got, below, to).start()
        grid_copy(12, 4, 2, low_got, above, to).start()
        return carry

    lax.fori_loop(0, HELPERS, grid_ghosts, 0)
    lax.fori_loop(1, HELPERS, grid_sends, 0)
    mine = pltpu.make_async_copy(
        grid_out.at[pl.ds(helper * 16 + 4, 8)], own_got.at[helper], own_sem
    )
    mine.start()
    mine.wait()
    pltpu.make_async_copy(high_got, high_got, grid_recv.at[1]).wait()
    pltpu.make_async_copy(low_got, low_got, grid_recv.at[2]).wait()
    seven = own_got.at[pl.ds(0, HELPERS - 1)]
    pltpu.make_async_copy(seven, seven, grid_recv.at[0]).wait()
    here = jnp.sum(own_got[...], axis=0)
    from_below = jnp.where(slab > 0, jnp.sum(low_got[...], axis=0), 0.0)
    from_above = jnp.where(slab < SLABS - 1, jnp.sum(high_got[...], axis=0), 0.0)
    grid_ref[...] = here + jnp.concatenate([from_below, from_above], axis=0)

    pltpu.make_async_copy(everything, everything, send_sem).wait()
    pltpu.make_async_copy(high_got, high_got, grid_send.at[1]).wait()
    pltpu.make_async_copy(low_got, low_got, grid_send.at[2]).wait()
    pltpu.make_async_copy(seven, seven, grid_send.at[0]).wait()
    for copy in stores:
        copy.wait()


def per_device(disp, strain, counts, assign, cached_pos, contact_mask, node_index, node_grads):
    vmem = pl.BlockSpec(memory_space=pltpu.VMEM)
    hbm = pl.BlockSpec(memory_space=pl.ANY)
    disp_out, stress, grid = pl.pallas_call(
        kernel,
        out_shape=(
            jax.ShapeDtypeStruct((FLAT, POINTS), F32),
            jax.ShapeDtypeStruct((9, POINTS), F32),
            jax.ShapeDtypeStruct((8, 128), F32),
        ),
        in_specs=[hbm, hbm, vmem, vmem, vmem, vmem, vmem, vmem],
        out_specs=(hbm, vmem, vmem),
        scratch_shapes=[
            pltpu.VMEM((FLAT, SLOTS), F32),
            pltpu.VMEM((DEVICES * ROWS, 128), F32),
            pltpu.VMEM((DEVICES * ROWS, 128), F32),
            pltpu.VMEM((GRAINS, 3 * POINTS), F32),
            pltpu.VMEM((GRAINS, 3 * POINTS), F32),
            pltpu.VMEM((128 * CHUNKS, POINTS), F32),
            pltpu.VMEM((GRAINS, GRAINS), BF16),
            pltpu.VMEM((GRAINS, POINTS), F32),
            pltpu.VMEM((GRAINS, 3 * POINTS), F32),
            pltpu.VMEM((128, 128), F32),
            pltpu.VMEM((HELPERS, 8, 128), F32),
            pltpu.VMEM((HELPERS, 4, 128), F32),
            pltpu.VMEM((HELPERS, 4, 128), F32),
            pltpu.SemaphoreType.DMA((4,)),
            pltpu.SemaphoreType.DMA,
            pltpu.SemaphoreType.DMA,
            pltpu.SemaphoreType.DMA,
            pltpu.SemaphoreType.DMA((3,)),
            pltpu.SemaphoreType.DMA((3,)),
            pltpu.SemaphoreType.DMA((3,)),
        ],
        compiler_params=pltpu.CompilerParams(
            collective_id=0, has_side_effects=True, vmem_limit_bytes=48 << 20
        ),
    )(
        cached_pos.transpose(1, 0, 2).reshape(FLAT, SLOTS),
        disp.transpose(1, 0, 2).reshape(FLAT, POINTS),
        contact_mask,
        strain,
        counts.reshape(1, POINTS),
        assign.reshape(1, POINTS),
        node_index,
        node_grads,
    )
    return (
        disp_out.reshape(3, GRAINS, POINTS).transpose(1, 0, 2),
        stress,
        grid.reshape(2, 4, 128)[:, :3].transpose(1, 0, 2),
    )


def solution(mesh):
    both = ("slab", "helper")
    return jax.shard_map(
        per_device,
        mesh=mesh,
        in_specs=(
            P(None, None, both),
            P(None, both),
            P(both),
            P(both, None),
            P(None, None, both),
            P(),
            P(None, both),
            P(None, None, both),
        ),
        out_specs=(P(None, None, both), P(None, both), P(None, "slab", "helper")),
        check_vma=False,
    )
```

```python
import itertools

import jax
import jax.numpy as jnp
from jax import lax
from jax.experimental import pallas as pl
from jax.experimental.pallas import tpu as pltpu
from jax.sharding import PartitionSpec as P

MESH = pl.DeviceIdType.MESH
GRAINS = 400
FLAT = 1200
POINTS = 128
WIDE = 3 * POINTS
SLOTS = 256
HELPERS = 8
SLABS = 16
DEVICES = 128
CHUNKS = 10
ROWS = 2 * CHUNKS
CORNERS = 8
BABY = 4
GIANT = 3
F32 = jnp.float32
BF16 = jnp.bfloat16


def halves(x):
    hi = x.astype(BF16)
    lo = (x - hi.astype(F32)).astype(BF16)
    return hi, lo


def dot(a, b):
    return jnp.dot(a, b, preferred_element_type=F32)


def dot3(a, b):
    return dot(a[0], b[0]) + dot(a[0], b[1]) + dot(a[1], b[0])


def dot_nt(a, b):
    return lax.dot_general(a, b, (((1,), (1,)), ((), ())), preferred_element_type=F32)


def ring(a):
    return min(a, 4 - a)


OFFSETS = sorted(
    (
        offset
        for offset in itertools.product(range(4), range(4), range(4), range(2))
        if any(offset)
    ),
    key=lambda o: (-ring(o[0]) - ring(o[1]) - ring(o[2]), (o[0] * 5 + o[1] * 11 + o[2] * 3 + o[3] * 7) % 13),
)


def kernel(
    cached_hbm, disp_hbm, mask_hbm, strain_hbm, counts_hbm, assign_hbm, node_hbm, grads_hbm,
    disp_out, stress_ref, grid_ref,
    cached, disp, mask, strain, counts_ref, assign, node, grads,
    sent, got, part, pos, steps_hi, steps_lo, giant_hi, giant_lo, hit, spread,
    grid_out, own_got, low_got, high_got,
    load_sem, send_sem, recv_sem, own_sem, grid_send, grid_recv,
):
    slab = lax.axis_index("slab")
    helper = lax.axis_index("helper")
    me = slab * HELPERS + helper

    moves = [(cached_hbm, cached)]
    for d in range(3):
        moves.append(
            (disp_hbm.at[pl.ds(d * GRAINS, GRAINS)], disp.at[:, pl.ds(d * POINTS, POINTS)])
        )
    moves += [
        (mask_hbm, mask), (strain_hbm, strain), (counts_hbm, counts_ref),
        (assign_hbm, assign), (node_hbm, node), (grads_hbm, grads),
    ]
    loads = [
        pltpu.make_async_copy(source, target, load_sem.at[i])
        for i, (source, target) in enumerate(moves)
    ]
    for copy in loads:
        copy.start()

    z, x, y, core = slab // 4, lax.rem(slab, 4), helper // 2, lax.rem(helper, 2)
    slab_at = {
        (a, b): lax.rem(z + a, 4) * 4 + lax.rem(x + b, 4) for a in range(4) for b in range(4)
    }
    helper_at = {
        (a, b): lax.rem(y + a, 4) * 2 + lax.rem(core + b, 2) for a in range(4) for b in range(2)
    }
    others = [(slab_at[o[:2]], helper_at[o[2:]]) for o in OFFSETS]

    barrier = pltpu.get_barrier_semaphore()
    for other in others:
        pl.semaphore_signal(barrier, inc=1, device_id=other, device_id_type=MESH)

    loads[0].wait()
    for k in range(CHUNKS):
        rows = min(128, FLAT - 128 * k)
        tile = cached[pl.ds(128 * k, rows), :]
        if rows < 128:
            tile = jnp.concatenate([tile, jnp.zeros((128 - rows, SLOTS), F32)], axis=0)
        sent[pl.ds(k, SLOTS, stride=CHUNKS), :] = tile.T

    pl.semaphore_wait(barrier, DEVICES - 1)

    for to_slab, to_helper in others:
        pltpu.make_async_remote_copy(
            src_ref=sent.at[pl.ds((to_slab * HELPERS + to_helper) * ROWS, ROWS)],
            dst_ref=got.at[pl.ds(me * ROWS, ROWS)],
            send_sem=send_sem,
            recv_sem=recv_sem,
            device_id=(to_slab, to_helper),
            device_id_type=MESH,
        ).start()
    own = pltpu.make_async_copy(
        sent.at[pl.ds(me * ROWS, ROWS)], got.at[pl.ds(me * ROWS, ROWS)], own_sem
    )
    own.start()

    for copy in loads[1:]:
        copy.wait()

    stiff = mask[...].astype(F32)
    scale = jnp.sum(stiff, axis=1, keepdims=True) + 1.0
    rate = 0.8 / scale
    rate_row = 0.8 / (jnp.sum(stiff, axis=0, keepdims=True) + 1.0)
    g_at = lax.broadcasted_iota(jnp.int32, (GRAINS, GRAINS), 0)
    h_at = lax.broadcasted_iota(jnp.int32, (GRAINS, GRAINS), 1)
    once = jnp.where(g_at == h_at, 0.2, 0.0) + rate * stiff
    once_h = halves(once)
    twice = dot3(once_h, once_h)
    twice_h = halves(twice)
    thrice = dot3(twice_h, once_h)
    hi, lo = halves(dot3(twice_h, twice_h))
    giant_hi[...] = hi
    giant_lo[...] = lo
    for i, power in enumerate((once, twice, thrice)):
        hi, lo = halves(power * rate_row)
        steps_hi[pl.ds(i * GRAINS, GRAINS), :] = hi
        steps_lo[pl.ds(i * GRAINS, GRAINS), :] = lo
    steps_hi[pl.ds(3 * GRAINS, GRAINS), :] = stiff.astype(BF16)

    def stepped(x_h, i):
        rows = pl.ds(i * GRAINS, GRAINS)
        return dot3((steps_hi[rows, :], steps_lo[rows, :]), x_h)

    def leap(x):
        return dot3((giant_hi[...], giant_lo[...]), halves(x))

    counts = jnp.concatenate([counts_ref[...]] * 3, axis=1)
    start = disp[...]
    start_h = halves(start * (1.25 * scale))
    powers = [start] + [stepped(start_h, i) for i in range(BABY - 1)]
    total = jnp.where(counts == BABY * GIANT, start, 0.0)
    for j in reversed(range(GIANT)):
        term = jnp.zeros((GRAINS, WIDE), F32)
        for i in range(BABY):
            term = jnp.where(counts == BABY * j + i, powers[i], term)
        total = term + leap(total)
    part[...] = total

    a_row = jnp.broadcast_to(assign[...], (POINTS, POINTS))
    a_col = a_row.T
    p_at = lax.broadcasted_iota(jnp.int32, (POINTS, POINTS), 0)
    q_at = lax.broadcasted_iota(jnp.int32, (POINTS, POINTS), 1)
    rank = jnp.sum(
        jnp.where((a_row == a_col) & (q_at < p_at), 1.0, 0.0), axis=1, keepdims=True
    ).astype(jnp.int32)
    column = a_col * 2 + rank
    column = jnp.concatenate([column, column], axis=1)
    slot_at = lax.broadcasted_iota(jnp.int32, (POINTS, SLOTS), 1)
    pick = jnp.where(column == slot_at, 1.0, 0.0).astype(BF16)

    for k in range(CORNERS):
        at = node[pl.ds(k, 1), :]
        layer = at // 1024
        target = lax.rem(at, 1024) // 128
        low = lax.rem(at, 128)
        lanes = pl.ds(k * POINTS, POINTS)
        spread[:, lanes] = jnp.where(p_at == low, 1.0, 0.0).astype(BF16)
        hit[:, lanes] = jnp.where(p_at // 4 == target * 4 + layer, 1.0, 0.0)

    everything = sent.at[pl.ds(0, (DEVICES - 1) * ROWS)]
    own.wait()
    pltpu.make_async_copy(everything, everything, recv_sem).wait()

    for k in range(CHUNKS):
        hi, lo = halves(got[pl.ds(k, SLOTS, stride=CHUNKS), :])
        tile = (dot(pick, hi) + dot(pick, lo)).T
        first = 128 * k
        while first < min(128 * k + 128, FLAT):
            e = first // GRAINS
            last = min(128 * k + 128, (e + 1) * GRAINS)
            pos[pl.ds(first - e * GRAINS, last - first), pl.ds(e * POINTS, POINTS)] = tile[
                first - 128 * k : last - 128 * k
            ]
            first = last

    place = pos[...]
    place_h = halves(place)
    powers = [rate * place] + [stepped(place_h, i) for i in range(BABY - 1)]
    contact = steps_hi[pl.ds(3 * GRAINS, GRAINS), :]
    pull = scale * place - (dot(contact, place_h[0]) + dot(contact, place_h[1]))
    total = None
    for j in reversed(range(GIANT)):
        term = jnp.zeros((GRAINS, WIDE), F32)
        for i in range(BABY):
            term = term + jnp.where(BABY * j + i < counts, powers[i], 0.0)
        total = term if total is None else term + leap(total)

    def across(x, e):
        return x[:, e * POINTS : (e + 1) * POINTS]

    relaxed = [
        part[:, pl.ds(d * POINTS, POINTS)]
        + sum(strain[pl.ds(3 * d + e, 1), :] * across(total, e) for e in range(3))
        for d in range(3)
    ]
    for d in range(3):
        disp_out[pl.ds(d * GRAINS, GRAINS), :] = relaxed[d]
    moments = [
        [jnp.sum(relaxed[d] * across(pull, e), axis=0, keepdims=True) / GRAINS for e in range(3)]
        for d in range(3)
    ]
    stress = [[0.5 * (moments[d][e] + moments[e][d]) for e in range(3)] for d in range(3)]
    for d in range(3):
        for e in range(3):
            stress_ref[pl.ds(3 * d + e, 1), :] = stress[d][e]

    nothing = jnp.zeros((1, POINTS), F32)
    rows = [
        jnp.concatenate([stress[0][d], stress[1][d], stress[2][d], nothing] * 2, axis=0)
        for d in range(3)
    ]
    contrib = jnp.concatenate(
        [-sum(rows[d] * grads[d, pl.ds(k, 1), :] for d in range(3)) for k in range(CORNERS)], axis=1
    )
    hi, lo = halves(jnp.concatenate([contrib] * 16, axis=0) * hit[...])
    grid_out[...] = dot_nt(hi, spread[...]) + dot_nt(lo, spread[...])
    below = lax.rem(slab + SLABS - 1, SLABS)
    above = lax.rem(slab + 1, SLABS)

    def grid_copy(first_row, count, kind, buffer, to_slab, to_helper):
        return pltpu.make_async_remote_copy(
            src_ref=grid_out.at[pl.ds(to_helper * 16 + first_row, count)],
            dst_ref=buffer.at[helper],
            send_sem=grid_send.at[kind],
            recv_sem=grid_recv.at[kind],
            device_id=(to_slab, to_helper),
            device_id_type=MESH,
        )

    for step in range(HELPERS):
        to = lax.rem(helper + step, HELPERS)
        grid_copy(0, 4, 1, high_got, below, to).start()
        grid_copy(12, 4, 2, low_got, above, to).start()
        if step:
            grid_copy(4, 8, 0, own_got, slab, to).start()
    mine = pltpu.make_async_copy(
        grid_out.at[pl.ds(helper * 16 + 4, 8)], own_got.at[helper], own_sem
    )
    mine.start()
    mine.wait()
    pltpu.make_async_copy(high_got, high_got, grid_recv.at[1]).wait()
    pltpu.make_async_copy(low_got, low_got, grid_recv.at[2]).wait()
    seven = own_got.at[pl.ds(0, HELPERS - 1)]
    pltpu.make_async_copy(seven, seven, grid_recv.at[0]).wait()
    here = jnp.sum(own_got[...], axis=0)
    from_below = jnp.where(slab > 0, jnp.sum(low_got[...], axis=0), 0.0)
    from_above = jnp.where(slab < SLABS - 1, jnp.sum(high_got[...], axis=0), 0.0)
    here = here + jnp.concatenate([from_below, from_above], axis=0)
    for c in range(3):
        for layer in range(2):
            grid_ref[c, pl.ds(layer, 1), :] = here[4 * layer + c : 4 * layer + c + 1]

    pltpu.make_async_copy(everything, everything, send_sem).wait()
    pltpu.make_async_copy(high_got, high_got, grid_send.at[1]).wait()
    pltpu.make_async_copy(low_got, low_got, grid_send.at[2]).wait()
    pltpu.make_async_copy(seven, seven, grid_send.at[0]).wait()


PIECES = 6


def hand_over(disp_in, stress_in, grid_in, disp_out, stress_out, grid_out, sems):
    rows = FLAT // PIECES
    copies = [
        pltpu.make_async_copy(
            disp_in.at[pl.ds(i * rows, rows)], disp_out.at[pl.ds(i * rows, rows)], sems.at[i]
        )
        for i in range(PIECES)
    ]
    copies.append(pltpu.make_async_copy(stress_in, stress_out, sems.at[PIECES]))
    copies.append(pltpu.make_async_copy(grid_in, grid_out, sems.at[PIECES + 1]))
    for copy in copies:
        copy.start()
    for copy in copies:
        copy.wait()


def per_device(disp, strain, counts, assign, cached_pos, contact_mask, node_index, node_grads):
    vmem = pl.BlockSpec(memory_space=pltpu.VMEM)
    hbm = pl.BlockSpec(memory_space=pltpu.MemorySpace.HBM)
    shapes = ((FLAT, POINTS), (9, POINTS), (3, 2, 128))

    def keep(x):
        return pltpu.with_memory_space_constraint(x, pltpu.MemorySpace.HBM)

    outs = pl.pallas_call(
        kernel,
        out_shape=tuple(pltpu.VMEM(shape, F32) for shape in shapes),
        in_specs=[hbm] * 8,
        out_specs=(vmem,) * 3,
        scratch_shapes=[
            pltpu.VMEM((FLAT, SLOTS), F32),
            pltpu.VMEM((GRAINS, WIDE), F32),
            pltpu.VMEM((GRAINS, GRAINS), jnp.int32),
            pltpu.VMEM((9, POINTS), F32),
            pltpu.VMEM((1, POINTS), jnp.int32),
            pltpu.VMEM((1, POINTS), jnp.int32),
            pltpu.VMEM((CORNERS, POINTS), jnp.int32),
            pltpu.VMEM((3, CORNERS, POINTS), F32),
            pltpu.VMEM((DEVICES * ROWS, 128), F32),
            pltpu.VMEM((DEVICES * ROWS, 128), F32),
            pltpu.VMEM((GRAINS, WIDE), F32),
            pltpu.VMEM((GRAINS, WIDE), F32),
            pltpu.VMEM((4 * GRAINS, GRAINS), BF16),
            pltpu.VMEM((3 * GRAINS, GRAINS), BF16),
            pltpu.VMEM((GRAINS, GRAINS), BF16),
            pltpu.VMEM((GRAINS, GRAINS), BF16),
            pltpu.VMEM((128, CORNERS * POINTS), F32),
            pltpu.VMEM((128, CORNERS * POINTS), BF16),
            pltpu.VMEM((128, 128), F32),
            pltpu.VMEM((HELPERS, 8, 128), F32),
            pltpu.VMEM((HELPERS, 4, 128), F32),
            pltpu.VMEM((HELPERS, 4, 128), F32),
            pltpu.SemaphoreType.DMA((10,)),
            pltpu.SemaphoreType.DMA,
            pltpu.SemaphoreType.DMA,
            pltpu.SemaphoreType.DMA,
            pltpu.SemaphoreType.DMA((3,)),
            pltpu.SemaphoreType.DMA((3,)),
        ],
        compiler_params=pltpu.CompilerParams(
            collective_id=0, has_side_effects=True, vmem_limit_bytes=56 << 20
        ),
    )(
        keep(cached_pos.transpose(1, 0, 2).reshape(FLAT, SLOTS)),
        keep(disp.transpose(1, 0, 2).reshape(FLAT, POINTS)),
        keep(contact_mask),
        keep(strain),
        keep(counts.reshape(1, POINTS)),
        keep(assign.reshape(1, POINTS)),
        keep(node_index),
        keep(node_grads),
    )
    disp_out, stress, grid = pl.pallas_call(
        hand_over,
        out_shape=tuple(jax.ShapeDtypeStruct(shape, F32) for shape in shapes),
        in_specs=[vmem] * 3,
        out_specs=(hbm,) * 3,
        scratch_shapes=[pltpu.SemaphoreType.DMA((PIECES + 2,))],
    )(*outs)
    return disp_out.reshape(3, GRAINS, POINTS).transpose(1, 0, 2), stress, grid


def solution(mesh):
    both = ("slab", "helper")
    return jax.shard_map(
        per_device,
        mesh=mesh,
        in_specs=(
            P(None, None, both),
            P(None, both),
            P(both),
            P(both, None),
            P(None, None, both),
            P(),
            P(None, both),
            P(None, None, both),
        ),
        out_specs=(P(None, None, both), P(None, both), P(None, "slab", "helper")),
        check_vma=False,
    )
```

```python
import itertools

import jax
import jax.numpy as jnp
from jax import lax
from jax.experimental import pallas as pl
from jax.experimental.pallas import tpu as pltpu
from jax.sharding import PartitionSpec as P

MESH = pl.DeviceIdType.MESH
GRAINS = 400
FLAT = 1200
POINTS = 128
WIDE = 3 * POINTS
SLOTS = 256
HELPERS = 8
SLABS = 16
DEVICES = 128
FULL = FLAT // 128
TAIL = FLAT - 128 * FULL
ROWS = 2 * FULL + 1
CORNERS = 8
BABY = 4
GIANT = 3
F32 = jnp.float32
BF16 = jnp.bfloat16


def halves(x):
    hi = x.astype(BF16)
    lo = (x - hi.astype(F32)).astype(BF16)
    return hi, lo


def dot(a, b):
    return jnp.dot(a, b, preferred_element_type=F32)


def dot2(a, b):
    width = b[0].shape[1]
    both = dot(a, jnp.concatenate(b, axis=1))
    return both[:, :width] + both[:, width:]


def dot3(a, b):
    return dot2(a[0], b) + dot(a[1], b[0])


def dot_nt(a, b):
    return lax.dot_general(a, b, (((1,), (1,)), ((), ())), preferred_element_type=F32)


def ring(a):
    return min(a, 4 - a)


OFFSETS = sorted(
    (
        offset
        for offset in itertools.product(range(4), range(4), range(4), range(2))
        if any(offset)
    ),
    key=lambda o: (-ring(o[0]) - ring(o[1]) - ring(o[2]), (o[0] * 5 + o[1] * 11 + o[2] * 3 + o[3] * 7) % 13),
)


def kernel(
    cached_hbm, disp_hbm, mask_hbm, strain_hbm, counts_hbm, assign_hbm, node_hbm, grads_hbm,
    disp_out, stress_ref, grid_ref,
    cached, disp, mask, strain, counts_ref, assign, node, grads,
    turned, sent, got, part, pos, steps_hi, steps_lo, giant_hi, giant_lo, hit, spread,
    grid_out, own_got, low_got, high_got,
    load_sem, send_sem, recv_sem, own_sem, grid_send, grid_recv,
):
    slab = lax.axis_index("slab")
    helper = lax.axis_index("helper")
    me = slab * HELPERS + helper

    moves = [(cached_hbm, cached)]
    for d in range(3):
        moves.append(
            (disp_hbm.at[pl.ds(d * GRAINS, GRAINS)], disp.at[:, pl.ds(d * POINTS, POINTS)])
        )
    moves += [
        (mask_hbm, mask), (strain_hbm, strain), (counts_hbm, counts_ref),
        (assign_hbm, assign), (node_hbm, node), (grads_hbm, grads),
    ]
    loads = [
        pltpu.make_async_copy(source, target, load_sem.at[i])
        for i, (source, target) in enumerate(moves)
    ]
    for copy in loads:
        copy.start()

    z, x, y, core = slab // 4, lax.rem(slab, 4), helper // 2, lax.rem(helper, 2)
    slab_at = {
        (a, b): lax.rem(z + a, 4) * 4 + lax.rem(x + b, 4) for a in range(4) for b in range(4)
    }
    helper_at = {
        (a, b): lax.rem(y + a, 4) * 2 + lax.rem(core + b, 2) for a in range(4) for b in range(2)
    }
    others = [(slab_at[o[:2]], helper_at[o[2:]]) for o in OFFSETS]

    barrier = pltpu.get_barrier_semaphore()
    for other in others:
        pl.semaphore_signal(barrier, inc=1, device_id=other, device_id_type=MESH)

    loads[0].wait()
    for k in range(FULL):
        turned[k] = cached[pl.ds(128 * k, 128), :].T
    for k in range(FULL):
        for c in range(2):
            sent[pl.ds(FULL * c + k, DEVICES, stride=ROWS), :] = turned[
                k, pl.ds(c, DEVICES, stride=2), :
            ]
    tail = cached[pl.ds(128 * FULL, TAIL), :]
    turned[0] = jnp.concatenate([tail, tail, jnp.zeros((128 - 2 * TAIL, SLOTS), F32)], axis=0).T
    lane = lax.broadcasted_iota(jnp.int32, (DEVICES, 128), 1)
    sent[pl.ds(2 * FULL, DEVICES, stride=ROWS), :] = jnp.where(
        lane < TAIL, turned[0, pl.ds(0, DEVICES, stride=2), :], turned[0, pl.ds(1, DEVICES, stride=2), :]
    )

    pl.semaphore_wait(barrier, DEVICES - 1)

    for to_slab, to_helper in others:
        pltpu.make_async_remote_copy(
            src_ref=sent.at[pl.ds((to_slab * HELPERS + to_helper) * ROWS, ROWS)],
            dst_ref=got.at[pl.ds(me * ROWS, ROWS)],
            send_sem=send_sem,
            recv_sem=recv_sem,
            device_id=(to_slab, to_helper),
            device_id_type=MESH,
        ).start()
    own = pltpu.make_async_copy(
        sent.at[pl.ds(me * ROWS, ROWS)], got.at[pl.ds(me * ROWS, ROWS)], own_sem
    )
    own.start()

    for copy in loads[1:]:
        copy.wait()

    stiff = mask[...].astype(F32)
    scale = jnp.sum(stiff, axis=1, keepdims=True) + 1.0
    rate = 0.8 / scale
    rate_row = 0.8 / (jnp.sum(stiff, axis=0, keepdims=True) + 1.0)
    g_at = lax.broadcasted_iota(jnp.int32, (GRAINS, GRAINS), 0)
    h_at = lax.broadcasted_iota(jnp.int32, (GRAINS, GRAINS), 1)
    once = jnp.where(g_at == h_at, 0.2, 0.0) + rate * stiff
    once_h = halves(once)
    twice = dot3(once_h, once_h)
    twice_h = halves(twice)
    thrice = dot3(twice_h, once_h)
    leap_h = halves(dot3(twice_h, twice_h))
    for i, power in enumerate((leap_h, halves(dot3(leap_h, leap_h)))):
        giant_hi[i] = power[0]
        giant_lo[i] = power[1]
    for i, power in enumerate((once, twice, thrice)):
        hi, lo = halves(power * rate_row)
        steps_hi[pl.ds(i * GRAINS, GRAINS), :] = hi
        steps_lo[pl.ds(i * GRAINS, GRAINS), :] = lo
    steps_hi[pl.ds(3 * GRAINS, GRAINS), :] = stiff.astype(BF16)

    def stepped(x_h, i):
        rows = pl.ds(i * GRAINS, GRAINS)
        return dot3((steps_hi[rows, :], steps_lo[rows, :]), x_h)

    def leap(i, x):
        return dot3((giant_hi[i], giant_lo[i]), halves(x))

    counts = jnp.concatenate([counts_ref[...]] * 3, axis=1)
    start = disp[...]
    start_h = halves(start * (1.25 * scale))
    powers = [start] + [stepped(start_h, i) for i in range(BABY - 1)]
    terms = []
    for j in range(GIANT):
        term = jnp.zeros((GRAINS, WIDE), F32)
        for i in range(BABY):
            term = jnp.where(counts == BABY * j + i, powers[i], term)
        terms.append(term)
    last = jnp.where(counts == BABY * GIANT, start, 0.0)
    part[...] = terms[0] + leap(0, terms[1] + leap(1, last)) + leap(1, terms[2])

    a_row = jnp.broadcast_to(assign[...], (POINTS, POINTS))
    a_col = a_row.T
    p_at = lax.broadcasted_iota(jnp.int32, (POINTS, POINTS), 0)
    q_at = lax.broadcasted_iota(jnp.int32, (POINTS, POINTS), 1)
    rank = jnp.sum(
        jnp.where((a_row == a_col) & (q_at < p_at), 1.0, 0.0), axis=1, keepdims=True
    ).astype(jnp.int32)
    column = rank * DEVICES + a_col
    column = jnp.concatenate([column, column], axis=1)
    slot_at = lax.broadcasted_iota(jnp.int32, (POINTS, SLOTS), 1)
    pick = jnp.where(column == slot_at, 1.0, 0.0).astype(BF16)

    for k in range(CORNERS):
        at = node[pl.ds(k, 1), :]
        layer = at // 1024
        target = lax.rem(at, 1024) // 128
        low = lax.rem(at, 128)
        lanes = pl.ds(k * POINTS, POINTS)
        spread[:, lanes] = jnp.where(p_at == low, 1.0, 0.0).astype(BF16)
        hit[:, lanes] = jnp.where(p_at // 4 == target * 4 + layer, 1.0, 0.0)

    everything = sent.at[pl.ds(0, (DEVICES - 1) * ROWS)]
    own.wait()
    pltpu.make_async_copy(everything, everything, recv_sem).wait()

    def chosen(slots, x):
        hi, lo = halves(x)
        return (dot(slots, hi) + dot(slots, lo)).T

    def settle(first, tile):
        last = first + tile.shape[0]
        at = first
        while at < last:
            e = at // GRAINS
            end = min(last, (e + 1) * GRAINS)
            pos[pl.ds(at - e * GRAINS, end - at), pl.ds(e * POINTS, POINTS)] = tile[
                at - first : end - first
            ]
            at = end

    for k in range(FULL):
        both = [got[pl.ds(FULL * c + k, DEVICES, stride=ROWS), :] for c in range(2)]
        settle(128 * k, chosen(pick, jnp.concatenate(both, axis=0)))
    tails = got[pl.ds(2 * FULL, DEVICES, stride=ROWS), :]
    settle(
        128 * FULL,
        chosen(pick[:, :DEVICES], tails)[:TAIL] + chosen(pick[:, DEVICES:], tails)[TAIL : 2 * TAIL],
    )

    place = pos[...]
    place_h = halves(place)
    powers = [rate * place] + [stepped(place_h, i) for i in range(BABY - 1)]
    contact = steps_hi[pl.ds(3 * GRAINS, GRAINS), :]
    pull = scale * place - dot2(contact, place_h)
    terms = []
    for j in range(GIANT):
        term = jnp.zeros((GRAINS, WIDE), F32)
        for i in range(BABY):
            term = term + jnp.where(BABY * j + i < counts, powers[i], 0.0)
        terms.append(term)
    total = terms[0] + leap(0, terms[1]) + leap(1, terms[2])

    def across(x, e):
        return x[:, e * POINTS : (e + 1) * POINTS]

    relaxed = [
        part[:, pl.ds(d * POINTS, POINTS)]
        + sum(strain[pl.ds(3 * d + e, 1), :] * across(total, e) for e in range(3))
        for d in range(3)
    ]
    for d in range(3):
        disp_out[pl.ds(d * GRAINS, GRAINS), :] = relaxed[d]
    moments = [
        [jnp.sum(relaxed[d] * across(pull, e), axis=0, keepdims=True) / GRAINS for e in range(3)]
        for d in range(3)
    ]
    stress = [[0.5 * (moments[d][e] + moments[e][d]) for e in range(3)] for d in range(3)]
    for d in range(3):
        for e in range(3):
            stress_ref[pl.ds(3 * d + e, 1), :] = stress[d][e]

    nothing = jnp.zeros((1, POINTS), F32)
    rows = [
        jnp.concatenate([stress[0][d], stress[1][d], stress[2][d], nothing] * 2, axis=0)
        for d in range(3)
    ]
    contrib = jnp.concatenate(
        [-sum(rows[d] * grads[d, pl.ds(k, 1), :] for d in range(3)) for k in range(CORNERS)], axis=1
    )
    hi, lo = halves(jnp.concatenate([contrib] * 16, axis=0) * hit[...])
    grid_out[...] = dot_nt(hi, spread[...]) + dot_nt(lo, spread[...])
    below = lax.rem(slab + SLABS - 1, SLABS)
    above = lax.rem(slab + 1, SLABS)

    def grid_copy(first_row, count, kind, buffer, to_slab, to_helper):
        return pltpu.make_async_remote_copy(
            src_ref=grid_out.at[pl.ds(to_helper * 16 + first_row, count)],
            dst_ref=buffer.at[helper],
            send_sem=grid_send.at[kind],
            recv_sem=grid_recv.at[kind],
            device_id=(to_slab, to_helper),
            device_id_type=MESH,
        )

    for step in (4, 5, 3, 2, 6, 7, 1, 0):
        to = lax.rem(helper + step, HELPERS)
        grid_copy(0, 4, 1, high_got, below, to).start()
        grid_copy(12, 4, 2, low_got, above, to).start()
        if step:
            grid_copy(4, 8, 0, own_got, slab, to).start()
    mine = pltpu.make_async_copy(
        grid_out.at[pl.ds(helper * 16 + 4, 8)], own_got.at[helper], own_sem
    )
    mine.start()
    mine.wait()
    pltpu.make_async_copy(high_got, high_got, grid_recv.at[1]).wait()
    pltpu.make_async_copy(low_got, low_got, grid_recv.at[2]).wait()
    seven = own_got.at[pl.ds(0, HELPERS - 1)]
    pltpu.make_async_copy(seven, seven, grid_recv.at[0]).wait()
    here = jnp.sum(own_got[...], axis=0)
    from_below = jnp.where(slab > 0, jnp.sum(low_got[...], axis=0), 0.0)
    from_above = jnp.where(slab < SLABS - 1, jnp.sum(high_got[...], axis=0), 0.0)
    here = here + jnp.concatenate([from_below, from_above], axis=0)
    for c in range(3):
        for layer in range(2):
            grid_ref[c, pl.ds(layer, 1), :] = here[4 * layer + c : 4 * layer + c + 1]

    pltpu.make_async_copy(everything, everything, send_sem).wait()
    pltpu.make_async_copy(high_got, high_got, grid_send.at[1]).wait()
    pltpu.make_async_copy(low_got, low_got, grid_send.at[2]).wait()
    pltpu.make_async_copy(seven, seven, grid_send.at[0]).wait()


PIECES = 6


def hand_over(disp_in, stress_in, grid_in, disp_out, stress_out, grid_out, sems):
    rows = FLAT // PIECES
    copies = [
        pltpu.make_async_copy(
            disp_in.at[pl.ds(i * rows, rows)], disp_out.at[pl.ds(i * rows, rows)], sems.at[i]
        )
        for i in range(PIECES)
    ]
    copies.append(pltpu.make_async_copy(stress_in, stress_out, sems.at[PIECES]))
    copies.append(pltpu.make_async_copy(grid_in, grid_out, sems.at[PIECES + 1]))
    for copy in copies:
        copy.start()
    for copy in copies:
        copy.wait()


def per_device(disp, strain, counts, assign, cached_pos, contact_mask, node_index, node_grads):
    vmem = pl.BlockSpec(memory_space=pltpu.VMEM)
    hbm = pl.BlockSpec(memory_space=pltpu.MemorySpace.HBM)
    shapes = ((FLAT, POINTS), (9, POINTS), (3, 2, 128))

    def keep(x):
        return pltpu.with_memory_space_constraint(x, pltpu.MemorySpace.HBM)

    outs = pl.pallas_call(
        kernel,
        out_shape=tuple(pltpu.VMEM(shape, F32) for shape in shapes),
        in_specs=[hbm] * 8,
        out_specs=(vmem,) * 3,
        scratch_shapes=[
            pltpu.VMEM((FLAT, SLOTS), F32),
            pltpu.VMEM((GRAINS, WIDE), F32),
            pltpu.VMEM((GRAINS, GRAINS), jnp.int32),
            pltpu.VMEM((9, POINTS), F32),
            pltpu.VMEM((1, POINTS), jnp.int32),
            pltpu.VMEM((1, POINTS), jnp.int32),
            pltpu.VMEM((CORNERS, POINTS), jnp.int32),
            pltpu.VMEM((3, CORNERS, POINTS), F32),
            pltpu.VMEM((FULL, SLOTS, 128), F32),
            pltpu.VMEM((DEVICES * ROWS, 128), F32),
            pltpu.VMEM((DEVICES * ROWS, 128), F32),
            pltpu.VMEM((GRAINS, WIDE), F32),
            pltpu.VMEM((GRAINS, WIDE), F32),
            pltpu.VMEM((4 * GRAINS, GRAINS), BF16),
            pltpu.VMEM((3 * GRAINS, GRAINS), BF16),
            pltpu.VMEM((2, GRAINS, GRAINS), BF16),
            pltpu.VMEM((2, GRAINS, GRAINS), BF16),
            pltpu.VMEM((128, CORNERS * POINTS), F32),
            pltpu.VMEM((128, CORNERS * POINTS), BF16),
            pltpu.VMEM((128, 128), F32),
            pltpu.VMEM((HELPERS, 8, 128), F32),
            pltpu.VMEM((HELPERS, 4, 128), F32),
            pltpu.VMEM((HELPERS, 4, 128), F32),
            pltpu.SemaphoreType.DMA((10,)),
            pltpu.SemaphoreType.DMA,
            pltpu.SemaphoreType.DMA,
            pltpu.SemaphoreType.DMA,
            pltpu.SemaphoreType.DMA((3,)),
            pltpu.SemaphoreType.DMA((3,)),
        ],
        compiler_params=pltpu.CompilerParams(
            collective_id=0, has_side_effects=True, vmem_limit_bytes=56 << 20
        ),
    )(
        keep(cached_pos.transpose(1, 0, 2).reshape(FLAT, SLOTS)),
        keep(disp.transpose(1, 0, 2).reshape(FLAT, POINTS)),
        keep(contact_mask),
        keep(strain),
        keep(counts.reshape(1, POINTS)),
        keep(assign.reshape(1, POINTS)),
        keep(node_index),
        keep(node_grads),
    )
    disp_out, stress, grid = pl.pallas_call(
        hand_over,
        out_shape=tuple(jax.ShapeDtypeStruct(shape, F32) for shape in shapes),
        in_specs=[vmem] * 3,
        out_specs=(hbm,) * 3,
        scratch_shapes=[pltpu.SemaphoreType.DMA((PIECES + 2,))],
        compiler_params=pltpu.CompilerParams(vmem_limit_bytes=8 << 20),
    )(*(pltpu.with_memory_space_constraint(x, pltpu.MemorySpace.VMEM) for x in outs))
    return disp_out.reshape(3, GRAINS, POINTS).transpose(1, 0, 2), stress, grid


def solution(mesh):
    both = ("slab", "helper")
    return jax.shard_map(
        per_device,
        mesh=mesh,
        in_specs=(
            P(None, None, both),
            P(None, both),
            P(both),
            P(both, None),
            P(None, None, both),
            P(),
            P(None, both),
            P(None, None, both),
        ),
        out_specs=(P(None, None, both), P(None, both), P(None, "slab", "helper")),
        check_vma=False,
    )
```

```python
import itertools

import jax
import jax.numpy as jnp
from jax import lax
from jax.experimental import pallas as pl
from jax.experimental.pallas import tpu as pltpu
from jax.sharding import PartitionSpec as P

MESH = pl.DeviceIdType.MESH
GRAINS = 400
FLAT = 1200
POINTS = 128
WIDE = 3 * POINTS
SLOTS = 256
HELPERS = 8
SLABS = 16
DEVICES = 128
HEAD = 256
REST = GRAINS - HEAD
TAIL = REST - 128
FIRST = 12
SECOND = 7
CORNERS = 8
BABY = 4
GIANT = 3
F32 = jnp.float32
BF16 = jnp.bfloat16


def halves(x):
    hi = x.astype(BF16)
    lo = (x - hi.astype(F32)).astype(BF16)
    return hi, lo


def dot(a, b):
    return jnp.dot(a, b, preferred_element_type=F32)


def dot2(a, b):
    width = b[0].shape[1]
    both = dot(a, jnp.concatenate(b, axis=1))
    return both[:, :width] + both[:, width:]


def dot3(a, b):
    return dot2(a[0], b) + dot(a[1], b[0])


def dot_nt(a, b):
    return lax.dot_general(a, b, (((1,), (1,)), ((), ())), preferred_element_type=F32)


def ring(a):
    return min(a, 4 - a)


OFFSETS = sorted(
    (
        offset
        for offset in itertools.product(range(4), range(4), range(4), range(2))
        if any(offset)
    ),
    key=lambda o: (-ring(o[0]) - ring(o[1]) - ring(o[2]), (o[0] * 5 + o[1] * 11 + o[2] * 3 + o[3] * 7) % 13),
)


def kernel(
    cached_hbm, disp_hbm, mask_hbm, strain_hbm, counts_hbm, assign_hbm, node_hbm, grads_hbm,
    disp_out, stress_ref, grid_ref,
    cached, disp, mask, strain, counts_ref, assign, node, grads,
    turned, sent_first, sent_second, got_first, got_second, part, pulled, pos, moved,
    steps_hi, steps_lo, contact, hit, spread,
    grid_out, own_got, low_got, high_got,
    load_sem, send_sem, recv_sem, own_sem, grid_own_sem, grid_send, grid_recv,
):
    slab = lax.axis_index("slab")
    helper = lax.axis_index("helper")
    me = slab * HELPERS + helper

    moves = [(cached_hbm, cached)]
    for d in range(3):
        moves.append(
            (disp_hbm.at[pl.ds(d * GRAINS, GRAINS)], disp.at[:, pl.ds(d * POINTS, POINTS)])
        )
    moves += [
        (mask_hbm, mask), (strain_hbm, strain), (counts_hbm, counts_ref),
        (assign_hbm, assign), (node_hbm, node), (grads_hbm, grads),
    ]
    loads = [
        pltpu.make_async_copy(source, target, load_sem.at[i])
        for i, (source, target) in enumerate(moves)
    ]
    for copy in loads:
        copy.start()

    z, x, y, core = slab // 4, lax.rem(slab, 4), helper // 2, lax.rem(helper, 2)
    slab_at = {
        (a, b): lax.rem(z + a, 4) * 4 + lax.rem(x + b, 4) for a in range(4) for b in range(4)
    }
    helper_at = {
        (a, b): lax.rem(y + a, 4) * 2 + lax.rem(core + b, 2) for a in range(4) for b in range(2)
    }
    others = [(slab_at[o[:2]], helper_at[o[2:]]) for o in OFFSETS]

    barrier = pltpu.get_barrier_semaphore()
    for other in others:
        pl.semaphore_signal(barrier, inc=1, device_id=other, device_id_type=MESH)

    @pl.when(slab == 0)
    def _():
        low_got[...] = jnp.zeros_like(low_got)

    @pl.when(slab == SLABS - 1)
    def _():
        high_got[...] = jnp.zeros_like(high_got)

    loads[0].wait()
    for e in range(3):
        for j in range(3):
            turned[3 * e + j] = cached[pl.ds(e * GRAINS + 128 * j, 128), :].T
    tail = [cached[pl.ds(e * GRAINS + GRAINS - TAIL, TAIL), :] for e in range(3)]
    turned[9] = jnp.concatenate(
        tail + tail + [jnp.zeros((128 - 6 * TAIL, SLOTS), F32)], axis=0
    ).T
    for c in range(2):
        mine = pl.ds(c, DEVICES, stride=2)
        for e in range(3):
            for j in range(2):
                sent_first[pl.ds(6 * c + 2 * e + j, DEVICES, stride=FIRST), :] = turned[
                    3 * e + j, mine, :
                ]
            sent_second[pl.ds(3 * c + e, DEVICES, stride=SECOND), :] = turned[3 * e + 2, mine, :]
    lane = lax.broadcasted_iota(jnp.int32, (DEVICES, 128), 1)
    sent_second[pl.ds(6, DEVICES, stride=SECOND), :] = jnp.where(
        lane < 3 * TAIL,
        turned[9, pl.ds(0, DEVICES, stride=2), :],
        turned[9, pl.ds(1, DEVICES, stride=2), :],
    )

    for copy in loads[1:]:
        copy.wait()
    stiff = mask[...].astype(F32)
    scale = jnp.sum(stiff, axis=1, keepdims=True) + 1.0
    rate = 0.8 / scale
    contact[...] = stiff.astype(BF16)

    def prepare():
        rate_row = 0.8 / (jnp.sum(mask[...].astype(F32), axis=0, keepdims=True) + 1.0)
        g_at = lax.broadcasted_iota(jnp.int32, (GRAINS, GRAINS), 0)
        h_at = lax.broadcasted_iota(jnp.int32, (GRAINS, GRAINS), 1)
        once = jnp.where(g_at == h_at, 0.2, 0.0) + rate * mask[...].astype(F32)

        def put(i, power):
            hi, lo = halves(power)
            steps_hi[pl.ds(i * GRAINS, GRAINS), :] = hi
            steps_lo[pl.ds(i * GRAINS, GRAINS), :] = lo
            return hi, lo

        def put_turned(i, power):
            put(i, power * (1.25 * scale) * rate_row)

        put_turned(0, once)
        once_h = halves(once)
        twice = dot3(once_h, once_h)
        put_turned(1, twice)
        twice_h = halves(twice)
        put_turned(2, dot3(twice_h, once_h))
        fourth_h = put(3, dot3(twice_h, twice_h))
        eighth_h = put(4, dot3(fourth_h, fourth_h))
        put(5, dot3(eighth_h, fourth_h))

    pl.semaphore_wait(barrier, DEVICES - 1)

    waves = ((sent_first, got_first, FIRST), (sent_second, got_second, SECOND))
    for wave, (sent, got, rows) in enumerate(waves):
        for to_slab, to_helper in others:
            pltpu.make_async_remote_copy(
                src_ref=sent.at[pl.ds((to_slab * HELPERS + to_helper) * rows, rows)],
                dst_ref=got.at[pl.ds(me * rows, rows)],
                send_sem=send_sem.at[wave],
                recv_sem=recv_sem.at[wave],
                device_id=(to_slab, to_helper),
                device_id_type=MESH,
            ).start()
    own = [
        pltpu.make_async_copy(
            sent.at[pl.ds(me * rows, rows)], got.at[pl.ds(me * rows, rows)], own_sem.at[wave]
        )
        for wave, (sent, got, rows) in enumerate(waves)
    ]
    for copy in own:
        copy.start()

    prepare()

    def step(i):
        rows = pl.ds(i * GRAINS, GRAINS)
        return steps_hi[rows, :], steps_lo[rows, :]

    def leap(i, x):
        return dot3(step(BABY - 2 + i), halves(x))

    counts = jnp.concatenate([counts_ref[...]] * 3, axis=1)
    start = disp[...]
    remainder, quarter = lax.rem(counts, BABY), counts // BABY

    def by(index, choices):
        value = choices[-1]
        for i in reversed(range(len(choices) - 1)):
            value = jnp.where(index == i, choices[i], value)
        return value

    start_h = halves(start * (1.25 * scale))
    moved_start = by(remainder, [start] + [rate * dot3(step(i), start_h) for i in range(BABY - 1)])
    terms = [jnp.where(quarter == j, moved_start, 0.0) for j in range(GIANT + 1)]
    free = terms[0] + leap(1, terms[1]) + leap(2, terms[2]) + leap(3, terms[3])
    part[...] = free
    pulled[...] = scale * free - dot2(contact[...], halves(free))

    a_row = jnp.broadcast_to(assign[...], (POINTS, POINTS))
    a_col = a_row.T
    p_at = lax.broadcasted_iota(jnp.int32, (POINTS, POINTS), 0)
    q_at = lax.broadcasted_iota(jnp.int32, (POINTS, POINTS), 1)
    rank = jnp.sum(
        jnp.where((a_row == a_col) & (q_at < p_at), 1.0, 0.0), axis=1, keepdims=True
    ).astype(jnp.int32)
    column = rank * DEVICES + a_col
    column = jnp.concatenate([column, column], axis=1)
    slot_at = lax.broadcasted_iota(jnp.int32, (POINTS, SLOTS), 1)
    pick = jnp.where(column == slot_at, 1.0, 0.0).astype(BF16)

    for k in range(CORNERS):
        at = node[pl.ds(k, 1), :]
        layer = at // 1024
        target = lax.rem(at, 1024) // 128
        low = lax.rem(at, 128)
        lanes = pl.ds(k * POINTS, POINTS)
        spread[:, lanes] = jnp.where(p_at == low, 1.0, 0.0).astype(BF16)
        hit[:, lanes] = jnp.where(p_at // 4 == target * 4 + layer, 1.0, 0.0)

    def chosen(slots, x):
        hi, lo = halves(x)
        return (dot(slots, hi) + dot(slots, lo)).T

    def arrived(wave):
        own[wave].wait()
        sent, _, rows = waves[wave]
        everything = sent.at[pl.ds(0, (DEVICES - 1) * rows)]
        pltpu.make_async_copy(everything, everything, recv_sem.at[wave]).wait()

    arrived(0)
    for e in range(3):
        for j in range(2):
            both = [
                got_first[pl.ds(6 * c + 2 * e + j, DEVICES, stride=FIRST), :] for c in range(2)
            ]
            pos[pl.ds(128 * j, 128), pl.ds(e * POINTS, POINTS)] = chosen(
                pick, jnp.concatenate(both, axis=0)
            )
    place_h = halves(pos[pl.ds(0, HEAD), :])
    for i in range(2 * BABY - 2):
        hi, lo = step(i)
        moved[pl.ds(i * GRAINS, GRAINS), :] = dot3((hi[:, :HEAD], lo[:, :HEAD]), place_h)

    arrived(1)
    for e in range(3):
        both = [got_second[pl.ds(3 * c + e, DEVICES, stride=SECOND), :] for c in range(2)]
        pos[pl.ds(HEAD, 128), pl.ds(e * POINTS, POINTS)] = chosen(
            pick, jnp.concatenate(both, axis=0)
        )
    tails = got_second[pl.ds(6, DEVICES, stride=SECOND), :]
    tails = (
        chosen(pick[:, :DEVICES], tails)[: 3 * TAIL]
        + chosen(pick[:, DEVICES:], tails)[3 * TAIL : 6 * TAIL]
    )
    for e in range(3):
        pos[pl.ds(HEAD + 128, TAIL), pl.ds(e * POINTS, POINTS)] = tails[e * TAIL : (e + 1) * TAIL]
    place_h = halves(pos[pl.ds(HEAD, REST), :])
    for i in range(2 * BABY - 2):
        hi, lo = step(i)
        rows = pl.ds(i * GRAINS, GRAINS)
        moved[rows, :] = moved[rows, :] + dot3((hi[:, HEAD:], lo[:, HEAD:]), place_h)

    def shifted(i):
        return moved[pl.ds(i * GRAINS, GRAINS), :]

    place = pos[...]
    inner = by(remainder, [place] + [shifted(i) for i in range(BABY - 1)])
    outer = by(quarter, [place] + [shifted(BABY - 1 + i) for i in range(GIANT)])

    def across(x, e):
        return x[:, e * POINTS : (e + 1) * POINTS]

    def over_grains(a, d, b, e):
        return jnp.sum(across(a, d) * across(b, e), axis=0, keepdims=True)

    overlap = [
        [over_grains(place, e, place, f) - over_grains(outer, e, inner, f) for f in range(3)]
        for e in range(3)
    ]
    moments = [
        [
            (
                over_grains(pulled[...], d, place, e)
                + sum(strain[pl.ds(3 * d + f, 1), :] * overlap[e][f] for f in range(3))
            )
            / GRAINS
            for e in range(3)
        ]
        for d in range(3)
    ]
    stress = [[0.5 * (moments[d][e] + moments[e][d]) for e in range(3)] for d in range(3)]
    for d in range(3):
        for e in range(3):
            stress_ref[pl.ds(3 * d + e, 1), :] = stress[d][e]

    nothing = jnp.zeros((1, POINTS), F32)
    rows = [
        jnp.concatenate([stress[0][d], stress[1][d], stress[2][d], nothing] * 2, axis=0)
        for d in range(3)
    ]
    contrib = jnp.concatenate(
        [-sum(rows[d] * grads[d, pl.ds(k, 1), :] for d in range(3)) for k in range(CORNERS)], axis=1
    )
    hi, lo = halves(jnp.concatenate([contrib] * 16, axis=0) * hit[...])
    grid_out[...] = dot_nt(hi, spread[...]) + dot_nt(lo, spread[...])
    def grid_copy(first_row, count, kind, buffer, to_slab, to_helper):
        return pltpu.make_async_remote_copy(
            src_ref=grid_out.at[pl.ds(to_helper * 16 + first_row, count)],
            dst_ref=buffer.at[helper],
            send_sem=grid_send.at[kind],
            recv_sem=grid_recv.at[kind],
            device_id=(to_slab, to_helper),
            device_id_type=MESH,
        )

    order = (4, 5, 3, 2, 6, 7, 1)

    @pl.when(slab > 0)
    def _():
        for ahead in order + (0,):
            grid_copy(0, 4, 1, high_got, slab - 1, lax.rem(helper + ahead, HELPERS)).start()

    for ahead in order:
        grid_copy(4, 8, 0, own_got, slab, lax.rem(helper + ahead, HELPERS)).start()

    @pl.when(slab < SLABS - 1)
    def _():
        for ahead in order + (0,):
            grid_copy(12, 4, 2, low_got, slab + 1, lax.rem(helper + ahead, HELPERS)).start()

    mine = pltpu.make_async_copy(
        grid_out.at[pl.ds(helper * 16 + 4, 8)], own_got.at[helper], grid_own_sem
    )
    mine.start()

    @pl.when(slab >= 0)
    def _():
        place = pos[...]
        powers = [rate * place] + [rate * shifted(i) for i in range(BABY - 1)]
        terms = []
        for j in range(GIANT):
            term = jnp.zeros((GRAINS, WIDE), F32)
            for i in range(BABY):
                term = term + jnp.where(BABY * j + i < counts, powers[i], 0.0)
            terms.append(term)
        total = terms[0] + leap(1, terms[1]) + leap(2, terms[2])
        for d in range(3):
            disp_out[pl.ds(d * GRAINS, GRAINS), :] = part[:, pl.ds(d * POINTS, POINTS)] + sum(
                strain[pl.ds(3 * d + e, 1), :] * across(total, e) for e in range(3)
            )

    mine.wait()

    @pl.when(slab < SLABS - 1)
    def _():
        pltpu.make_async_copy(high_got, high_got, grid_recv.at[1]).wait()

    @pl.when(slab > 0)
    def _():
        pltpu.make_async_copy(low_got, low_got, grid_recv.at[2]).wait()

    seven = own_got.at[pl.ds(0, HELPERS - 1)]
    pltpu.make_async_copy(seven, seven, grid_recv.at[0]).wait()
    here = jnp.sum(own_got[...], axis=0)
    from_below, from_above = jnp.sum(low_got[...], axis=0), jnp.sum(high_got[...], axis=0)
    here = here + jnp.concatenate([from_below, from_above], axis=0)
    for c in range(3):
        for layer in range(2):
            grid_ref[c, pl.ds(layer, 1), :] = here[4 * layer + c : 4 * layer + c + 1]

    for wave, (sent, _, rows) in enumerate(waves):
        everything = sent.at[pl.ds(0, (DEVICES - 1) * rows)]
        pltpu.make_async_copy(everything, everything, send_sem.at[wave]).wait()

    @pl.when(slab > 0)
    def _():
        pltpu.make_async_copy(high_got, high_got, grid_send.at[1]).wait()

    @pl.when(slab < SLABS - 1)
    def _():
        pltpu.make_async_copy(low_got, low_got, grid_send.at[2]).wait()

    pltpu.make_async_copy(seven, seven, grid_send.at[0]).wait()


PIECES = 6


def hand_over(disp_in, stress_in, grid_in, disp_out, stress_out, grid_out, sems):
    rows = FLAT // PIECES
    copies = [
        pltpu.make_async_copy(
            disp_in.at[pl.ds(i * rows, rows)], disp_out.at[pl.ds(i * rows, rows)], sems.at[i]
        )
        for i in range(PIECES)
    ]
    copies.append(pltpu.make_async_copy(stress_in, stress_out, sems.at[PIECES]))
    copies.append(pltpu.make_async_copy(grid_in, grid_out, sems.at[PIECES + 1]))
    for copy in copies:
        copy.start()
    for copy in copies:
        copy.wait()


def per_device(disp, strain, counts, assign, cached_pos, contact_mask, node_index, node_grads):
    vmem = pl.BlockSpec(memory_space=pltpu.VMEM)
    hbm = pl.BlockSpec(memory_space=pltpu.MemorySpace.HBM)
    shapes = ((FLAT, POINTS), (9, POINTS), (3, 2, 128))

    def keep(x):
        return pltpu.with_memory_space_constraint(x, pltpu.MemorySpace.HBM)

    outs = pl.pallas_call(
        kernel,
        out_shape=tuple(pltpu.VMEM(shape, F32) for shape in shapes),
        in_specs=[hbm] * 8,
        out_specs=(vmem,) * 3,
        scratch_shapes=[
            pltpu.VMEM((FLAT, SLOTS), F32),
            pltpu.VMEM((GRAINS, WIDE), F32),
            pltpu.VMEM((GRAINS, GRAINS), jnp.int32),
            pltpu.VMEM((9, POINTS), F32),
            pltpu.VMEM((1, POINTS), jnp.int32),
            pltpu.VMEM((1, POINTS), jnp.int32),
            pltpu.VMEM((CORNERS, POINTS), jnp.int32),
            pltpu.VMEM((3, CORNERS, POINTS), F32),
            pltpu.VMEM((10, SLOTS, 128), F32),
            pltpu.VMEM((DEVICES * FIRST, 128), F32),
            pltpu.VMEM((DEVICES * SECOND, 128), F32),
            pltpu.VMEM((DEVICES * FIRST, 128), F32),
            pltpu.VMEM((DEVICES * SECOND, 128), F32),
            pltpu.VMEM((GRAINS, WIDE), F32),
            pltpu.VMEM((GRAINS, WIDE), F32),
            pltpu.VMEM((GRAINS, WIDE), F32),
            pltpu.VMEM((6 * GRAINS, WIDE), F32),
            pltpu.VMEM((6 * GRAINS, GRAINS), BF16),
            pltpu.VMEM((6 * GRAINS, GRAINS), BF16),
            pltpu.VMEM((GRAINS, GRAINS), BF16),
            pltpu.VMEM((128, CORNERS * POINTS), F32),
            pltpu.VMEM((128, CORNERS * POINTS), BF16),
            pltpu.VMEM((128, 128), F32),
            pltpu.VMEM((HELPERS, 8, 128), F32),
            pltpu.VMEM((HELPERS, 4, 128), F32),
            pltpu.VMEM((HELPERS, 4, 128), F32),
            pltpu.SemaphoreType.DMA((10,)),
            pltpu.SemaphoreType.DMA((2,)),
            pltpu.SemaphoreType.DMA((2,)),
            pltpu.SemaphoreType.DMA((2,)),
            pltpu.SemaphoreType.DMA,
            pltpu.SemaphoreType.DMA((3,)),
            pltpu.SemaphoreType.DMA((3,)),
        ],
        compiler_params=pltpu.CompilerParams(
            collective_id=0, has_side_effects=True, vmem_limit_bytes=56 << 20
        ),
    )(
        keep(cached_pos.transpose(1, 0, 2).reshape(FLAT, SLOTS)),
        keep(disp.transpose(1, 0, 2).reshape(FLAT, POINTS)),
        keep(contact_mask),
        keep(strain),
        keep(counts.reshape(1, POINTS)),
        keep(assign.reshape(1, POINTS)),
        keep(node_index),
        keep(node_grads),
    )
    disp_out, stress, grid = pl.pallas_call(
        hand_over,
        out_shape=tuple(jax.ShapeDtypeStruct(shape, F32) for shape in shapes),
        in_specs=[vmem] * 3,
        out_specs=(hbm,) * 3,
        scratch_shapes=[pltpu.SemaphoreType.DMA((PIECES + 2,))],
        compiler_params=pltpu.CompilerParams(vmem_limit_bytes=8 << 20),
    )(*(pltpu.with_memory_space_constraint(x, pltpu.MemorySpace.VMEM) for x in outs))
    return disp_out.reshape(3, GRAINS, POINTS).transpose(1, 0, 2), stress, grid


def solution(mesh):
    both = ("slab", "helper")
    return jax.shard_map(
        per_device,
        mesh=mesh,
        in_specs=(
            P(None, None, both),
            P(None, both),
            P(both),
            P(both, None),
            P(None, None, both),
            P(),
            P(None, both),
            P(None, None, both),
        ),
        out_specs=(P(None, None, both), P(None, both), P(None, "slab", "helper")),
        check_vma=False,
    )
```

```python
import itertools
import random

import jax
import jax.numpy as jnp
from jax import lax
from jax.experimental import pallas as pl
from jax.experimental.pallas import tpu as pltpu
from jax.sharding import PartitionSpec as P

MESH = pl.DeviceIdType.MESH
GRAINS = 400
FLAT = 1200
POINTS = 128
WIDE = 3 * POINTS
SLOTS = 256
HELPERS = 8
SLABS = 16
DEVICES = 128
HEAD = 256
REST = GRAINS - HEAD
TAIL = REST - 128
FIRST = 12
SECOND = 7
CORNERS = 8
BABY = 4
GIANT = 3
F32 = jnp.float32
BF16 = jnp.bfloat16


def halves(x):
    hi = x.astype(BF16)
    lo = (x - hi.astype(F32)).astype(BF16)
    return hi, lo


def dot(a, b):
    return jnp.dot(a, b, preferred_element_type=F32)


def dot2(a, b):
    width = b[0].shape[1]
    both = dot(a, jnp.concatenate(b, axis=1))
    return both[:, :width] + both[:, width:]


def dot3(a, b):
    return dot2(a[0], b) + dot(a[1], b[0])


def dot_nt(a, b):
    return lax.dot_general(a, b, (((1,), (1,)), ((), ())), preferred_element_type=F32)


def ring(a):
    return min(a, 4 - a)


def hops(offset):
    return ring(offset[0]) + ring(offset[1]) + ring(offset[2])


SHUFFLED = [
    offset for offset in itertools.product(range(4), range(4), range(4), range(2)) if any(offset)
]
random.Random(1).shuffle(SHUFFLED)
FARTHEST = sorted(SHUFFLED, key=lambda offset: -hops(offset))


def in_plane(offset):
    return 0 in offset[:3]


NEAR = [offset for offset in FARTHEST if in_plane(offset)]
ORDERS = (sorted(SHUFFLED, key=lambda offset: not in_plane(offset)), FARTHEST)


def kernel(
    cached_hbm, disp_hbm, mask_hbm, strain_hbm, counts_hbm, assign_hbm, node_hbm, grads_hbm,
    disp_out, stress_ref, grid_ref,
    cached, disp, mask, strain, counts_ref, assign, node, grads,
    turned, sent_first, sent_second, got_first, got_second, part, pulled, pos, met,
    steps_hi, steps_lo, first_hi, first_lo, second_hi, second_lo, contact, hit, spread,
    grid_out, own_got, low_got, high_got,
    load_sem, line_sem, send_sem, recv_sem, own_sem, grid_own_sem, grid_send, grid_recv,
):
    slab = lax.axis_index("slab")
    helper = lax.axis_index("helper")
    me = slab * HELPERS + helper

    moves = [(cached_hbm, cached)]
    for d in range(3):
        moves.append(
            (disp_hbm.at[pl.ds(d * GRAINS, GRAINS)], disp.at[:, pl.ds(d * POINTS, POINTS)])
        )
    moves += [
        (mask_hbm, mask), (strain_hbm, strain), (counts_hbm, counts_ref),
        (assign_hbm, assign), (node_hbm, node), (grads_hbm, grads),
    ]
    loads = [
        pltpu.make_async_copy(source, target, load_sem.at[i])
        for i, (source, target) in enumerate(moves)
    ]
    for copy in loads:
        copy.start()

    z, x, y, core = slab // 4, lax.rem(slab, 4), helper // 2, lax.rem(helper, 2)
    slab_at = {
        (a, b): lax.rem(z + a, 4) * 4 + lax.rem(x + b, 4) for a in range(4) for b in range(4)
    }
    helper_at = {
        (a, b): lax.rem(y + a, 4) * 2 + lax.rem(core + b, 2) for a in range(4) for b in range(2)
    }

    def at(offset):
        return slab_at[offset[:2]], helper_at[offset[2:]]

    barrier = pltpu.get_barrier_semaphore()
    for offset in NEAR:
        pl.semaphore_signal(barrier, inc=1, device_id=at(offset), device_id_type=MESH)

    @pl.when(slab == 0)
    def _():
        low_got[...] = jnp.zeros_like(low_got)

    @pl.when(slab == SLABS - 1)
    def _():
        high_got[...] = jnp.zeros_like(high_got)

    loads[0].wait()
    for e in range(3):
        for j in range(3):
            turned[3 * e + j] = cached[pl.ds(e * GRAINS + 128 * j, 128), :].T
    tail = [cached[pl.ds(e * GRAINS + GRAINS - TAIL, TAIL), :] for e in range(3)]
    turned[9] = jnp.concatenate(
        tail + tail + [jnp.zeros((128 - 6 * TAIL, SLOTS), F32)], axis=0
    ).T
    for c in range(2):
        mine = pl.ds(c, DEVICES, stride=2)
        for e in range(3):
            for j in range(2):
                sent_first[pl.ds(6 * c + 2 * e + j, DEVICES, stride=FIRST), :] = turned[
                    3 * e + j, mine, :
                ]
            sent_second[pl.ds(3 * c + e, DEVICES, stride=SECOND), :] = turned[3 * e + 2, mine, :]
    lane = lax.broadcasted_iota(jnp.int32, (DEVICES, 128), 1)
    sent_second[pl.ds(6, DEVICES, stride=SECOND), :] = jnp.where(
        lane < 3 * TAIL,
        turned[9, pl.ds(0, DEVICES, stride=2), :],
        turned[9, pl.ds(1, DEVICES, stride=2), :],
    )

    for copy in loads[1:]:
        copy.wait()
    stiff = mask[...].astype(F32)
    scale = jnp.sum(stiff, axis=1, keepdims=True) + 1.0
    rate = 0.8 / scale
    contact[...] = stiff.astype(BF16)

    def prepare():
        rate_row = 0.8 / (jnp.sum(mask[...].astype(F32), axis=0, keepdims=True) + 1.0)
        g_at = lax.broadcasted_iota(jnp.int32, (GRAINS, GRAINS), 0)
        h_at = lax.broadcasted_iota(jnp.int32, (GRAINS, GRAINS), 1)
        once = jnp.where(g_at == h_at, 0.2, 0.0) + rate * mask[...].astype(F32)

        def put(i, power):
            hi, lo = halves(power)
            steps_hi[pl.ds(i * GRAINS, GRAINS), :] = hi
            steps_lo[pl.ds(i * GRAINS, GRAINS), :] = lo
            side, at = i // GIANT, i % GIANT
            first_hi[side, :, pl.ds(at * HEAD, HEAD)] = hi[:, :HEAD]
            first_lo[side, :, pl.ds(at * HEAD, HEAD)] = lo[:, :HEAD]
            second_hi[side, :, pl.ds(at * REST, REST)] = hi[:, HEAD:]
            second_lo[side, :, pl.ds(at * REST, REST)] = lo[:, HEAD:]
            return hi, lo

        def put_turned(i, power):
            put(i, power * (1.25 * scale) * rate_row)

        put_turned(0, once)
        once_h = halves(once)
        twice = dot3(once_h, once_h)
        put_turned(1, twice)
        twice_h = halves(twice)
        put_turned(2, dot3(twice_h, once_h))
        fourth_h = put(3, dot3(twice_h, twice_h))
        eighth_h = put(4, dot3(fourth_h, fourth_h))
        put(5, dot3(eighth_h, fourth_h))

    pl.semaphore_wait(barrier, len(NEAR))
    for a in (2, 1, 3):
        pl.semaphore_signal(line_sem, inc=1, device_id=at((a, 0, 0, 0)), device_id_type=MESH)

    waves = ((sent_first, got_first, FIRST), (sent_second, got_second, SECOND))
    for wave, (sent, got, rows) in enumerate(waves):
        for i, offset in enumerate(ORDERS[wave]):
            if wave == 0 and i == len(NEAR):
                pl.semaphore_wait(line_sem, 3)
            to_slab, to_helper = at(offset)
            pltpu.make_async_remote_copy(
                src_ref=sent.at[pl.ds((to_slab * HELPERS + to_helper) * rows, rows)],
                dst_ref=got.at[pl.ds(me * rows, rows)],
                send_sem=send_sem.at[wave],
                recv_sem=recv_sem.at[wave],
                device_id=(to_slab, to_helper),
                device_id_type=MESH,
            ).start()
    own = [
        pltpu.make_async_copy(
            sent.at[pl.ds(me * rows, rows)], got.at[pl.ds(me * rows, rows)], own_sem.at[wave]
        )
        for wave, (sent, got, rows) in enumerate(waves)
    ]
    for copy in own:
        copy.start()

    prepare()

    def step(i):
        rows = pl.ds(i * GRAINS, GRAINS)
        return steps_hi[rows, :], steps_lo[rows, :]

    def leap(i, x):
        return dot3(step(BABY - 2 + i), halves(x))

    counts = jnp.concatenate([counts_ref[...]] * 3, axis=1)
    start = disp[...]
    remainder, quarter = lax.rem(counts, BABY), counts // BABY

    def by(index, choices):
        value = choices[-1]
        for i in reversed(range(len(choices) - 1)):
            value = jnp.where(index == i, choices[i], value)
        return value

    start_h = halves(start * (1.25 * scale))
    moved_start = by(remainder, [start] + [rate * dot3(step(i), start_h) for i in range(BABY - 1)])
    terms = [jnp.where(quarter == j, moved_start, 0.0) for j in range(GIANT + 1)]
    free = terms[0] + leap(1, terms[1]) + leap(2, terms[2]) + leap(3, terms[3])
    part[...] = free
    pulled[...] = scale * free - dot2(contact[...], halves(free))

    a_row = jnp.broadcast_to(assign[...], (POINTS, POINTS))
    a_col = a_row.T
    p_at = lax.broadcasted_iota(jnp.int32, (POINTS, POINTS), 0)
    q_at = lax.broadcasted_iota(jnp.int32, (POINTS, POINTS), 1)
    rank = jnp.sum(
        jnp.where((a_row == a_col) & (q_at < p_at), 1.0, 0.0), axis=1, keepdims=True
    ).astype(jnp.int32)
    column = rank * DEVICES + a_col
    column = jnp.concatenate([column, column], axis=1)
    slot_at = lax.broadcasted_iota(jnp.int32, (POINTS, SLOTS), 1)
    pick = jnp.where(column == slot_at, 1.0, 0.0).astype(BF16)

    for k in range(CORNERS):
        value = node[pl.ds(k, 1), :]
        layer = value // 1024
        target = lax.rem(value, 1024) // 128
        low = lax.rem(value, 128)
        lanes = pl.ds(k * POINTS, POINTS)
        spread[:, lanes] = jnp.where(p_at == low, 1.0, 0.0).astype(BF16)
        hit[:, lanes] = jnp.where(p_at // 4 == target * 4 + layer, 1.0, 0.0)

    def chosen(slots, x):
        hi, lo = halves(x)
        return (dot(slots, hi) + dot(slots, lo)).T

    def arrived(wave):
        own[wave].wait()
        sent, _, rows = waves[wave]
        everything = sent.at[pl.ds(0, (DEVICES - 1) * rows)]
        pltpu.make_async_copy(everything, everything, recv_sem.at[wave]).wait()

    def masked(index, x_h):
        keeps = [jnp.where(index == i + 1, 1.0, 0.0).astype(BF16) for i in range(GIANT)]
        return [jnp.concatenate([x * keep for keep in keeps], axis=0) for x in x_h]

    arrived(0)
    for e in range(3):
        for j in range(2):
            both = [
                got_first[pl.ds(6 * c + 2 * e + j, DEVICES, stride=FIRST), :] for c in range(2)
            ]
            pos[pl.ds(128 * j, 128), pl.ds(e * POINTS, POINTS)] = chosen(
                pick, jnp.concatenate(both, axis=0)
            )
    place_h = halves(pos[pl.ds(0, HEAD), :])
    sides = (remainder, quarter)
    for side, index in enumerate(sides):
        met[side] = dot3((first_hi[side], first_lo[side]), masked(index, place_h))

    arrived(1)
    for e in range(3):
        both = [got_second[pl.ds(3 * c + e, DEVICES, stride=SECOND), :] for c in range(2)]
        pos[pl.ds(HEAD, 128), pl.ds(e * POINTS, POINTS)] = chosen(
            pick, jnp.concatenate(both, axis=0)
        )
    tails = got_second[pl.ds(6, DEVICES, stride=SECOND), :]
    tails = (
        chosen(pick[:, :DEVICES], tails)[: 3 * TAIL]
        + chosen(pick[:, DEVICES:], tails)[3 * TAIL : 6 * TAIL]
    )
    for e in range(3):
        pos[pl.ds(HEAD + 128, TAIL), pl.ds(e * POINTS, POINTS)] = tails[e * TAIL : (e + 1) * TAIL]
    place_h = halves(pos[pl.ds(HEAD, REST), :])
    place = pos[...]
    inner, outer = [
        jnp.where(index == 0, place, met[side])
        + dot3((second_hi[side], second_lo[side]), masked(index, place_h))
        for side, index in enumerate(sides)
    ]

    def across(x, e):
        return x[:, e * POINTS : (e + 1) * POINTS]

    def over_grains(a, d, b, e):
        return jnp.sum(across(a, d) * across(b, e), axis=0, keepdims=True)

    overlap = [
        [over_grains(place, e, place, f) - over_grains(outer, e, inner, f) for f in range(3)]
        for e in range(3)
    ]
    moments = [
        [
            (
                over_grains(pulled[...], d, place, e)
                + sum(strain[pl.ds(3 * d + f, 1), :] * overlap[e][f] for f in range(3))
            )
            / GRAINS
            for e in range(3)
        ]
        for d in range(3)
    ]
    stress = [[0.5 * (moments[d][e] + moments[e][d]) for e in range(3)] for d in range(3)]
    for d in range(3):
        for e in range(3):
            stress_ref[pl.ds(3 * d + e, 1), :] = stress[d][e]

    nothing = jnp.zeros((1, POINTS), F32)
    rows = [
        jnp.concatenate([stress[0][d], stress[1][d], stress[2][d], nothing] * 2, axis=0)
        for d in range(3)
    ]
    contrib = jnp.concatenate(
        [-sum(rows[d] * grads[d, pl.ds(k, 1), :] for d in range(3)) for k in range(CORNERS)], axis=1
    )
    hi, lo = halves(jnp.concatenate([contrib] * 16, axis=0) * hit[...])
    grid_out[...] = dot_nt(hi, spread[...]) + dot_nt(lo, spread[...])
    def grid_copy(first_row, count, kind, buffer, to_slab, to_helper):
        return pltpu.make_async_remote_copy(
            src_ref=grid_out.at[pl.ds(to_helper * 16 + first_row, count)],
            dst_ref=buffer.at[helper],
            send_sem=grid_send.at[kind],
            recv_sem=grid_recv.at[kind],
            device_id=(to_slab, to_helper),
            device_id_type=MESH,
        )

    order = (4, 5, 3, 2, 6, 7, 1)

    @pl.when(slab > 0)
    def _():
        for ahead in order + (0,):
            grid_copy(0, 4, 1, high_got, slab - 1, lax.rem(helper + ahead, HELPERS)).start()

    for ahead in order:
        grid_copy(4, 8, 0, own_got, slab, lax.rem(helper + ahead, HELPERS)).start()

    @pl.when(slab < SLABS - 1)
    def _():
        for ahead in order + (0,):
            grid_copy(12, 4, 2, low_got, slab + 1, lax.rem(helper + ahead, HELPERS)).start()

    mine = pltpu.make_async_copy(
        grid_out.at[pl.ds(helper * 16 + 4, 8)], own_got.at[helper], grid_own_sem
    )
    mine.start()

    @pl.when(slab >= 0)
    def _():
        place = pos[...]
        place_h = halves(place)
        powers = [rate * place] + [rate * dot3(step(i), place_h) for i in range(BABY - 1)]
        terms = []
        for j in range(GIANT):
            term = jnp.zeros((GRAINS, WIDE), F32)
            for i in range(BABY):
                term = term + jnp.where(BABY * j + i < counts, powers[i], 0.0)
            terms.append(term)
        total = terms[0] + leap(1, terms[1]) + leap(2, terms[2])
        for d in range(3):
            disp_out[pl.ds(d * GRAINS, GRAINS), :] = part[:, pl.ds(d * POINTS, POINTS)] + sum(
                strain[pl.ds(3 * d + e, 1), :] * across(total, e) for e in range(3)
            )

    mine.wait()

    @pl.when(slab < SLABS - 1)
    def _():
        pltpu.make_async_copy(high_got, high_got, grid_recv.at[1]).wait()

    @pl.when(slab > 0)
    def _():
        pltpu.make_async_copy(low_got, low_got, grid_recv.at[2]).wait()

    seven = own_got.at[pl.ds(0, HELPERS - 1)]
    pltpu.make_async_copy(seven, seven, grid_recv.at[0]).wait()
    here = jnp.sum(own_got[...], axis=0)
    from_below, from_above = jnp.sum(low_got[...], axis=0), jnp.sum(high_got[...], axis=0)
    here = here + jnp.concatenate([from_below, from_above], axis=0)
    for c in range(3):
        for layer in range(2):
            grid_ref[c, pl.ds(layer, 1), :] = here[4 * layer + c : 4 * layer + c + 1]

    for wave, (sent, _, rows) in enumerate(waves):
        everything = sent.at[pl.ds(0, (DEVICES - 1) * rows)]
        pltpu.make_async_copy(everything, everything, send_sem.at[wave]).wait()

    @pl.when(slab > 0)
    def _():
        pltpu.make_async_copy(high_got, high_got, grid_send.at[1]).wait()

    @pl.when(slab < SLABS - 1)
    def _():
        pltpu.make_async_copy(low_got, low_got, grid_send.at[2]).wait()

    pltpu.make_async_copy(seven, seven, grid_send.at[0]).wait()


PIECES = 6


def hand_over(disp_in, stress_in, grid_in, disp_out, stress_out, grid_out, sems):
    rows = FLAT // PIECES
    copies = [
        pltpu.make_async_copy(
            disp_in.at[pl.ds(i * rows, rows)], disp_out.at[pl.ds(i * rows, rows)], sems.at[i]
        )
        for i in range(PIECES)
    ]
    copies.append(pltpu.make_async_copy(stress_in, stress_out, sems.at[PIECES]))
    copies.append(pltpu.make_async_copy(grid_in, grid_out, sems.at[PIECES + 1]))
    for copy in copies:
        copy.start()
    for copy in copies:
        copy.wait()


def per_device(disp, strain, counts, assign, cached_pos, contact_mask, node_index, node_grads):
    vmem = pl.BlockSpec(memory_space=pltpu.VMEM)
    hbm = pl.BlockSpec(memory_space=pltpu.MemorySpace.HBM)
    shapes = ((FLAT, POINTS), (9, POINTS), (3, 2, 128))

    def keep(x):
        return pltpu.with_memory_space_constraint(x, pltpu.MemorySpace.HBM)

    outs = pl.pallas_call(
        kernel,
        out_shape=tuple(pltpu.VMEM(shape, F32) for shape in shapes),
        in_specs=[hbm] * 8,
        out_specs=(vmem,) * 3,
        scratch_shapes=[
            pltpu.VMEM((FLAT, SLOTS), F32),
            pltpu.VMEM((GRAINS, WIDE), F32),
            pltpu.VMEM((GRAINS, GRAINS), jnp.int32),
            pltpu.VMEM((9, POINTS), F32),
            pltpu.VMEM((1, POINTS), jnp.int32),
            pltpu.VMEM((1, POINTS), jnp.int32),
            pltpu.VMEM((CORNERS, POINTS), jnp.int32),
            pltpu.VMEM((3, CORNERS, POINTS), F32),
            pltpu.VMEM((10, SLOTS, 128), F32),
            pltpu.VMEM((DEVICES * FIRST, 128), F32),
            pltpu.VMEM((DEVICES * SECOND, 128), F32),
            pltpu.VMEM((DEVICES * FIRST, 128), F32),
            pltpu.VMEM((DEVICES * SECOND, 128), F32),
            pltpu.VMEM((GRAINS, WIDE), F32),
            pltpu.VMEM((GRAINS, WIDE), F32),
            pltpu.VMEM((GRAINS, WIDE), F32),
            pltpu.VMEM((2, GRAINS, WIDE), F32),
            pltpu.VMEM((6 * GRAINS, GRAINS), BF16),
            pltpu.VMEM((6 * GRAINS, GRAINS), BF16),
            pltpu.VMEM((2, GRAINS, GIANT * HEAD), BF16),
            pltpu.VMEM((2, GRAINS, GIANT * HEAD), BF16),
            pltpu.VMEM((2, GRAINS, GIANT * REST), BF16),
            pltpu.VMEM((2, GRAINS, GIANT * REST), BF16),
            pltpu.VMEM((GRAINS, GRAINS), BF16),
            pltpu.VMEM((128, CORNERS * POINTS), F32),
            pltpu.VMEM((128, CORNERS * POINTS), BF16),
            pltpu.VMEM((128, 128), F32),
            pltpu.VMEM((HELPERS, 8, 128), F32),
            pltpu.VMEM((HELPERS, 4, 128), F32),
            pltpu.VMEM((HELPERS, 4, 128), F32),
            pltpu.SemaphoreType.DMA((10,)),
            pltpu.SemaphoreType.REGULAR,
            pltpu.SemaphoreType.DMA((2,)),
            pltpu.SemaphoreType.DMA((2,)),
            pltpu.SemaphoreType.DMA((2,)),
            pltpu.SemaphoreType.DMA,
            pltpu.SemaphoreType.DMA((3,)),
            pltpu.SemaphoreType.DMA((3,)),
        ],
        compiler_params=pltpu.CompilerParams(
            collective_id=0, has_side_effects=True, vmem_limit_bytes=56 << 20
        ),
    )(
        keep(cached_pos.transpose(1, 0, 2).reshape(FLAT, SLOTS)),
        keep(disp.transpose(1, 0, 2).reshape(FLAT, POINTS)),
        keep(contact_mask),
        keep(strain),
        keep(counts.reshape(1, POINTS)),
        keep(assign.reshape(1, POINTS)),
        keep(node_index),
        keep(node_grads),
    )
    disp_out, stress, grid = pl.pallas_call(
        hand_over,
        out_shape=tuple(jax.ShapeDtypeStruct(shape, F32) for shape in shapes),
        in_specs=[vmem] * 3,
        out_specs=(hbm,) * 3,
        scratch_shapes=[pltpu.SemaphoreType.DMA((PIECES + 2,))],
        compiler_params=pltpu.CompilerParams(vmem_limit_bytes=8 << 20),
    )(*(pltpu.with_memory_space_constraint(x, pltpu.MemorySpace.VMEM) for x in outs))
    return disp_out.reshape(3, GRAINS, POINTS).transpose(1, 0, 2), stress, grid


def solution(mesh):
    both = ("slab", "helper")
    return jax.shard_map(
        per_device,
        mesh=mesh,
        in_specs=(
            P(None, None, both),
            P(None, both),
            P(both),
            P(both, None),
            P(None, None, both),
            P(),
            P(None, both),
            P(None, None, both),
        ),
        out_specs=(P(None, None, both), P(None, both), P(None, "slab", "helper")),
        check_vma=False,
    )
```

```python
import itertools
import random

import jax
import jax.numpy as jnp
from jax import lax
from jax.experimental import pallas as pl
from jax.experimental.pallas import tpu as pltpu
from jax.sharding import PartitionSpec as P

MESH = pl.DeviceIdType.MESH
GRAINS = 400
FLAT = 1200
POINTS = 128
WIDE = 3 * POINTS
SLOTS = 256
HELPERS = 8
SLABS = 16
DEVICES = 128
HEAD = 256
REST = GRAINS - HEAD
TAIL = REST - 128
FIRST = 12
SECOND = 7
CORNERS = 8
BABY = 4
GIANT = 3
F32 = jnp.float32
BF16 = jnp.bfloat16


def halves(x):
    hi = x.astype(BF16)
    lo = (x - hi.astype(F32)).astype(BF16)
    return hi, lo


def dot(a, b):
    return jnp.dot(a, b, preferred_element_type=F32)


def dot2(a, b):
    width = b[0].shape[1]
    both = dot(a, jnp.concatenate(b, axis=1))
    return both[:, :width] + both[:, width:]


def dot3(a, b):
    return dot2(a[0], b) + dot(a[1], b[0])


def dot_nt(a, b):
    return lax.dot_general(a, b, (((1,), (1,)), ((), ())), preferred_element_type=F32)


def ring(a):
    return min(a, 4 - a)


def hops(offset):
    return ring(offset[0]) + ring(offset[1]) + ring(offset[2])


SHUFFLED = [
    offset for offset in itertools.product(range(4), range(4), range(4), range(2)) if any(offset)
]
random.Random(1).shuffle(SHUFFLED)
FARTHEST = sorted(SHUFFLED, key=lambda offset: -hops(offset))


def in_plane(offset):
    return 0 in offset[:3]


NEAR = [offset for offset in FARTHEST if in_plane(offset)]
ORDERS = (sorted(SHUFFLED, key=lambda offset: not in_plane(offset)), FARTHEST)


def kernel(
    cached_hbm, disp_hbm, mask_hbm, strain_hbm, counts_hbm, assign_hbm, node_hbm, grads_hbm,
    disp_out, stress_ref, grid_ref,
    cached, disp, mask, strain, counts_ref, assign, node, grads,
    turned, sent_first, sent_second, got_first, got_second, part, pulled, pos, met,
    steps_hi, steps_lo, first_hi, first_lo, second_hi, second_lo, contact, hit, spread,
    grid_out, own_got, low_got, high_got,
    load_sem, line_sem, send_sem, recv_sem, own_sem, grid_own_sem, grid_send, grid_recv,
):
    slab = lax.axis_index("slab")
    helper = lax.axis_index("helper")
    me = slab * HELPERS + helper

    moves = [(cached_hbm, cached)]
    for d in range(3):
        moves.append(
            (disp_hbm.at[pl.ds(d * GRAINS, GRAINS)], disp.at[:, pl.ds(d * POINTS, POINTS)])
        )
    moves += [
        (mask_hbm, mask), (strain_hbm, strain), (counts_hbm, counts_ref),
        (assign_hbm, assign), (node_hbm, node), (grads_hbm, grads),
    ]
    loads = [
        pltpu.make_async_copy(source, target, load_sem.at[i])
        for i, (source, target) in enumerate(moves)
    ]
    for copy in loads:
        copy.start()

    z, x, y, core = slab // 4, lax.rem(slab, 4), helper // 2, lax.rem(helper, 2)
    slab_at = {
        (a, b): lax.rem(z + a, 4) * 4 + lax.rem(x + b, 4) for a in range(4) for b in range(4)
    }
    helper_at = {
        (a, b): lax.rem(y + a, 4) * 2 + lax.rem(core + b, 2) for a in range(4) for b in range(2)
    }

    def at(offset):
        return slab_at[offset[:2]], helper_at[offset[2:]]

    barrier = pltpu.get_barrier_semaphore()
    for offset in NEAR:
        pl.semaphore_signal(barrier, inc=1, device_id=at(offset), device_id_type=MESH)

    @pl.when(slab == 0)
    def _():
        low_got[...] = jnp.zeros_like(low_got)

    @pl.when(slab == SLABS - 1)
    def _():
        high_got[...] = jnp.zeros_like(high_got)

    loads[0].wait()
    for e in range(3):
        for j in range(3):
            turned[3 * e + j] = cached[pl.ds(e * GRAINS + 128 * j, 128), :].T
    tail = [cached[pl.ds(e * GRAINS + GRAINS - TAIL, TAIL), :] for e in range(3)]
    turned[9] = jnp.concatenate(
        tail + tail + [jnp.zeros((128 - 6 * TAIL, SLOTS), F32)], axis=0
    ).T
    for c in range(2):
        mine = pl.ds(c, DEVICES, stride=2)
        for e in range(3):
            for j in range(2):
                sent_first[pl.ds(6 * c + 2 * e + j, DEVICES, stride=FIRST), :] = turned[
                    3 * e + j, mine, :
                ]
            sent_second[pl.ds(3 * c + e, DEVICES, stride=SECOND), :] = turned[3 * e + 2, mine, :]
    lane = lax.broadcasted_iota(jnp.int32, (DEVICES, 128), 1)
    sent_second[pl.ds(6, DEVICES, stride=SECOND), :] = jnp.where(
        lane < 3 * TAIL,
        turned[9, pl.ds(0, DEVICES, stride=2), :],
        turned[9, pl.ds(1, DEVICES, stride=2), :],
    )

    for copy in loads[1:]:
        copy.wait()
    stiff = mask[...].astype(F32)
    scale = jnp.sum(stiff, axis=1, keepdims=True) + 1.0
    rate = 0.8 / scale
    contact[...] = stiff.astype(BF16)

    def prepare():
        rate_row = 0.8 / (jnp.sum(mask[...].astype(F32), axis=0, keepdims=True) + 1.0)
        g_at = lax.broadcasted_iota(jnp.int32, (GRAINS, GRAINS), 0)
        h_at = lax.broadcasted_iota(jnp.int32, (GRAINS, GRAINS), 1)
        once = jnp.where(g_at == h_at, 0.2, 0.0) + rate * mask[...].astype(F32)

        def put(i, power):
            hi, lo = halves(power)
            steps_hi[pl.ds(i * GRAINS, GRAINS), :] = hi
            steps_lo[pl.ds(i * GRAINS, GRAINS), :] = lo
            side, at = i // GIANT, i % GIANT
            first_hi[side, :, pl.ds(at * HEAD, HEAD)] = hi[:, :HEAD]
            first_lo[side, :, pl.ds(at * HEAD, HEAD)] = lo[:, :HEAD]
            second_hi[side, :, pl.ds(at * REST, REST)] = hi[:, HEAD:]
            second_lo[side, :, pl.ds(at * REST, REST)] = lo[:, HEAD:]
            return hi, lo

        def put_turned(i, power):
            put(i, power * (1.25 * scale) * rate_row)

        put_turned(0, once)
        once_h = halves(once)
        twice = dot3(once_h, once_h)
        put_turned(1, twice)
        twice_h = halves(twice)
        put_turned(2, dot3(twice_h, once_h))
        fourth_h = put(3, dot3(twice_h, twice_h))
        eighth_h = put(4, dot3(fourth_h, fourth_h))
        put(5, dot3(eighth_h, fourth_h))

    pl.semaphore_wait(barrier, len(NEAR))
    for a in (2, 1, 3):
        pl.semaphore_signal(line_sem, inc=1, device_id=at((a, 0, 0, 0)), device_id_type=MESH)

    waves = ((sent_first, got_first, FIRST), (sent_second, got_second, SECOND))
    for wave, (sent, got, rows) in enumerate(waves):
        for i, offset in enumerate(ORDERS[wave]):
            if wave == 0 and i == len(NEAR):
                pl.semaphore_wait(line_sem, 3)
            to_slab, to_helper = at(offset)
            pltpu.make_async_remote_copy(
                src_ref=sent.at[pl.ds((to_slab * HELPERS + to_helper) * rows, rows)],
                dst_ref=got.at[pl.ds(me * rows, rows)],
                send_sem=send_sem.at[wave],
                recv_sem=recv_sem.at[wave],
                device_id=(to_slab, to_helper),
                device_id_type=MESH,
            ).start()
    own = [
        pltpu.make_async_copy(
            sent.at[pl.ds(me * rows, rows)], got.at[pl.ds(me * rows, rows)], own_sem.at[wave]
        )
        for wave, (sent, got, rows) in enumerate(waves)
    ]
    for copy in own:
        copy.start()

    prepare()

    def step(i):
        rows = pl.ds(i * GRAINS, GRAINS)
        return steps_hi[rows, :], steps_lo[rows, :]

    def leap(i, x):
        return dot3(step(BABY - 2 + i), halves(x))

    counts = jnp.concatenate([counts_ref[...]] * 3, axis=1)
    start = disp[...]
    remainder, quarter = lax.rem(counts, BABY), counts // BABY

    sides = (remainder, quarter)

    def masked(index, x_h):
        keeps = [jnp.where(index == i + 1, 1.0, 0.0).astype(BF16) for i in range(GIANT)]
        return [jnp.concatenate([x * keep for keep in keeps], axis=0) for x in x_h]

    def first_part(side, x_h):
        return dot3((first_hi[side], first_lo[side]), masked(sides[side], x_h))

    def second_part(side, x_h):
        return dot3((second_hi[side], second_lo[side]), masked(sides[side], x_h))

    def whole(side, x):
        return first_part(side, halves(x[:HEAD])) + second_part(side, halves(x[HEAD:]))

    free = jnp.where(remainder == 0, start, rate * whole(0, start * (1.25 * scale)))
    free = jnp.where(quarter == 0, free, whole(1, free))
    part[...] = free
    pulled[...] = scale * free - dot2(contact[...], halves(free))

    a_row = jnp.broadcast_to(assign[...], (POINTS, POINTS))
    a_col = a_row.T
    p_at = lax.broadcasted_iota(jnp.int32, (POINTS, POINTS), 0)
    q_at = lax.broadcasted_iota(jnp.int32, (POINTS, POINTS), 1)
    rank = jnp.sum(
        jnp.where((a_row == a_col) & (q_at < p_at), 1.0, 0.0), axis=1, keepdims=True
    ).astype(jnp.int32)
    column = rank * DEVICES + a_col
    column = jnp.concatenate([column, column], axis=1)
    slot_at = lax.broadcasted_iota(jnp.int32, (POINTS, SLOTS), 1)
    pick = jnp.where(column == slot_at, 1.0, 0.0).astype(BF16)

    for k in range(CORNERS):
        value = node[pl.ds(k, 1), :]
        layer = value // 1024
        target = lax.rem(value, 1024) // 128
        low = lax.rem(value, 128)
        lanes = pl.ds(k * POINTS, POINTS)
        spread[:, lanes] = jnp.where(p_at == low, 1.0, 0.0).astype(BF16)
        hit[:, lanes] = jnp.where(p_at // 4 == target * 4 + layer, 1.0, 0.0)

    def chosen(slots, x):
        hi, lo = halves(x)
        return (dot(slots, hi) + dot(slots, lo)).T

    def arrived(wave):
        own[wave].wait()
        sent, _, rows = waves[wave]
        everything = sent.at[pl.ds(0, (DEVICES - 1) * rows)]
        pltpu.make_async_copy(everything, everything, recv_sem.at[wave]).wait()

    arrived(0)
    for e in range(3):
        for j in range(2):
            both = [
                got_first[pl.ds(6 * c + 2 * e + j, DEVICES, stride=FIRST), :] for c in range(2)
            ]
            pos[pl.ds(128 * j, 128), pl.ds(e * POINTS, POINTS)] = chosen(
                pick, jnp.concatenate(both, axis=0)
            )
    place_h = halves(pos[pl.ds(0, HEAD), :])
    for side in range(2):
        met[side] = first_part(side, place_h)

    arrived(1)
    for e in range(3):
        both = [got_second[pl.ds(3 * c + e, DEVICES, stride=SECOND), :] for c in range(2)]
        pos[pl.ds(HEAD, 128), pl.ds(e * POINTS, POINTS)] = chosen(
            pick, jnp.concatenate(both, axis=0)
        )
    tails = got_second[pl.ds(6, DEVICES, stride=SECOND), :]
    tails = (
        chosen(pick[:, :DEVICES], tails)[: 3 * TAIL]
        + chosen(pick[:, DEVICES:], tails)[3 * TAIL : 6 * TAIL]
    )
    for e in range(3):
        pos[pl.ds(HEAD + 128, TAIL), pl.ds(e * POINTS, POINTS)] = tails[e * TAIL : (e + 1) * TAIL]
    place_h = halves(pos[pl.ds(HEAD, REST), :])
    place = pos[...]
    inner, outer = [
        jnp.where(index == 0, place, met[side]) + second_part(side, place_h)
        for side, index in enumerate(sides)
    ]

    def across(x, e):
        return x[:, e * POINTS : (e + 1) * POINTS]

    def over_grains(a, d, b, e):
        return jnp.sum(across(a, d) * across(b, e), axis=0, keepdims=True)

    overlap = [
        [over_grains(place, e, place, f) - over_grains(outer, e, inner, f) for f in range(3)]
        for e in range(3)
    ]
    moments = [
        [
            (
                over_grains(pulled[...], d, place, e)
                + sum(strain[pl.ds(3 * d + f, 1), :] * overlap[e][f] for f in range(3))
            )
            / GRAINS
            for e in range(3)
        ]
        for d in range(3)
    ]
    stress = [[0.5 * (moments[d][e] + moments[e][d]) for e in range(3)] for d in range(3)]
    for d in range(3):
        for e in range(3):
            stress_ref[pl.ds(3 * d + e, 1), :] = stress[d][e]

    nothing = jnp.zeros((1, POINTS), F32)
    rows = [
        jnp.concatenate([stress[0][d], stress[1][d], stress[2][d], nothing] * 2, axis=0)
        for d in range(3)
    ]
    contrib = jnp.concatenate(
        [-sum(rows[d] * grads[d, pl.ds(k, 1), :] for d in range(3)) for k in range(CORNERS)], axis=1
    )
    hi, lo = halves(jnp.concatenate([contrib] * 16, axis=0) * hit[...])
    grid_out[...] = dot_nt(hi, spread[...]) + dot_nt(lo, spread[...])
    def grid_copy(first_row, count, kind, buffer, to_slab, to_helper):
        return pltpu.make_async_remote_copy(
            src_ref=grid_out.at[pl.ds(to_helper * 16 + first_row, count)],
            dst_ref=buffer.at[helper],
            send_sem=grid_send.at[kind],
            recv_sem=grid_recv.at[kind],
            device_id=(to_slab, to_helper),
            device_id_type=MESH,
        )

    order = (4, 5, 3, 2, 6, 7, 1)

    @pl.when(slab > 0)
    def _():
        for ahead in order + (0,):
            grid_copy(0, 4, 1, high_got, slab - 1, lax.rem(helper + ahead, HELPERS)).start()

    for ahead in order:
        grid_copy(4, 8, 0, own_got, slab, lax.rem(helper + ahead, HELPERS)).start()

    @pl.when(slab < SLABS - 1)
    def _():
        for ahead in order + (0,):
            grid_copy(12, 4, 2, low_got, slab + 1, lax.rem(helper + ahead, HELPERS)).start()

    mine = pltpu.make_async_copy(
        grid_out.at[pl.ds(helper * 16 + 4, 8)], own_got.at[helper], grid_own_sem
    )
    mine.start()

    @pl.when(slab >= 0)
    def _():
        place = pos[...]
        place_h = halves(place)
        powers = [rate * place] + [rate * dot3(step(i), place_h) for i in range(BABY - 1)]
        terms = []
        for j in range(GIANT):
            term = jnp.zeros((GRAINS, WIDE), F32)
            for i in range(BABY):
                term = term + jnp.where(BABY * j + i < counts, powers[i], 0.0)
            terms.append(term)
        total = terms[0] + leap(1, terms[1]) + leap(2, terms[2])
        for d in range(3):
            disp_out[pl.ds(d * GRAINS, GRAINS), :] = part[:, pl.ds(d * POINTS, POINTS)] + sum(
                strain[pl.ds(3 * d + e, 1), :] * across(total, e) for e in range(3)
            )

    mine.wait()

    @pl.when(slab < SLABS - 1)
    def _():
        pltpu.make_async_copy(high_got, high_got, grid_recv.at[1]).wait()

    @pl.when(slab > 0)
    def _():
        pltpu.make_async_copy(low_got, low_got, grid_recv.at[2]).wait()

    seven = own_got.at[pl.ds(0, HELPERS - 1)]
    pltpu.make_async_copy(seven, seven, grid_recv.at[0]).wait()
    here = jnp.sum(own_got[...], axis=0)
    from_below, from_above = jnp.sum(low_got[...], axis=0), jnp.sum(high_got[...], axis=0)
    here = here + jnp.concatenate([from_below, from_above], axis=0)
    for c in range(3):
        for layer in range(2):
            grid_ref[c, pl.ds(layer, 1), :] = here[4 * layer + c : 4 * layer + c + 1]

    for wave, (sent, _, rows) in enumerate(waves):
        everything = sent.at[pl.ds(0, (DEVICES - 1) * rows)]
        pltpu.make_async_copy(everything, everything, send_sem.at[wave]).wait()

    @pl.when(slab > 0)
    def _():
        pltpu.make_async_copy(high_got, high_got, grid_send.at[1]).wait()

    @pl.when(slab < SLABS - 1)
    def _():
        pltpu.make_async_copy(low_got, low_got, grid_send.at[2]).wait()

    pltpu.make_async_copy(seven, seven, grid_send.at[0]).wait()


PIECES = 6


def hand_over(disp_in, stress_in, grid_in, disp_out, stress_out, grid_out, sems):
    rows = FLAT // PIECES
    copies = [
        pltpu.make_async_copy(
            disp_in.at[pl.ds(i * rows, rows)], disp_out.at[pl.ds(i * rows, rows)], sems.at[i]
        )
        for i in range(PIECES)
    ]
    copies.append(pltpu.make_async_copy(stress_in, stress_out, sems.at[PIECES]))
    copies.append(pltpu.make_async_copy(grid_in, grid_out, sems.at[PIECES + 1]))
    for copy in copies:
        copy.start()
    for copy in copies:
        copy.wait()


def per_device(disp, strain, counts, assign, cached_pos, contact_mask, node_index, node_grads):
    vmem = pl.BlockSpec(memory_space=pltpu.VMEM)
    hbm = pl.BlockSpec(memory_space=pltpu.MemorySpace.HBM)
    shapes = ((FLAT, POINTS), (9, POINTS), (3, 2, 128))

    def keep(x):
        return pltpu.with_memory_space_constraint(x, pltpu.MemorySpace.HBM)

    outs = pl.pallas_call(
        kernel,
        out_shape=tuple(pltpu.VMEM(shape, F32) for shape in shapes),
        in_specs=[hbm] * 8,
        out_specs=(vmem,) * 3,
        scratch_shapes=[
            pltpu.VMEM((FLAT, SLOTS), F32),
            pltpu.VMEM((GRAINS, WIDE), F32),
            pltpu.VMEM((GRAINS, GRAINS), jnp.int32),
            pltpu.VMEM((9, POINTS), F32),
            pltpu.VMEM((1, POINTS), jnp.int32),
            pltpu.VMEM((1, POINTS), jnp.int32),
            pltpu.VMEM((CORNERS, POINTS), jnp.int32),
            pltpu.VMEM((3, CORNERS, POINTS), F32),
            pltpu.VMEM((10, SLOTS, 128), F32),
            pltpu.VMEM((DEVICES * FIRST, 128), F32),
            pltpu.VMEM((DEVICES * SECOND, 128), F32),
            pltpu.VMEM((DEVICES * FIRST, 128), F32),
            pltpu.VMEM((DEVICES * SECOND, 128), F32),
            pltpu.VMEM((GRAINS, WIDE), F32),
            pltpu.VMEM((GRAINS, WIDE), F32),
            pltpu.VMEM((GRAINS, WIDE), F32),
            pltpu.VMEM((2, GRAINS, WIDE), F32),
            pltpu.VMEM((6 * GRAINS, GRAINS), BF16),
            pltpu.VMEM((6 * GRAINS, GRAINS), BF16),
            pltpu.VMEM((2, GRAINS, GIANT * HEAD), BF16),
            pltpu.VMEM((2, GRAINS, GIANT * HEAD), BF16),
            pltpu.VMEM((2, GRAINS, GIANT * REST), BF16),
            pltpu.VMEM((2, GRAINS, GIANT * REST), BF16),
            pltpu.VMEM((GRAINS, GRAINS), BF16),
            pltpu.VMEM((128, CORNERS * POINTS), F32),
            pltpu.VMEM((128, CORNERS * POINTS), BF16),
            pltpu.VMEM((128, 128), F32),
            pltpu.VMEM((HELPERS, 8, 128), F32),
            pltpu.VMEM((HELPERS, 4, 128), F32),
            pltpu.VMEM((HELPERS, 4, 128), F32),
            pltpu.SemaphoreType.DMA((10,)),
            pltpu.SemaphoreType.REGULAR,
            pltpu.SemaphoreType.DMA((2,)),
            pltpu.SemaphoreType.DMA((2,)),
            pltpu.SemaphoreType.DMA((2,)),
            pltpu.SemaphoreType.DMA,
            pltpu.SemaphoreType.DMA((3,)),
            pltpu.SemaphoreType.DMA((3,)),
        ],
        compiler_params=pltpu.CompilerParams(
            collective_id=0, has_side_effects=True, vmem_limit_bytes=56 << 20
        ),
    )(
        keep(cached_pos.transpose(1, 0, 2).reshape(FLAT, SLOTS)),
        keep(disp.transpose(1, 0, 2).reshape(FLAT, POINTS)),
        keep(contact_mask),
        keep(strain),
        keep(counts.reshape(1, POINTS)),
        keep(assign.reshape(1, POINTS)),
        keep(node_index),
        keep(node_grads),
    )
    disp_out, stress, grid = pl.pallas_call(
        hand_over,
        out_shape=tuple(jax.ShapeDtypeStruct(shape, F32) for shape in shapes),
        in_specs=[vmem] * 3,
        out_specs=(hbm,) * 3,
        scratch_shapes=[pltpu.SemaphoreType.DMA((PIECES + 2,))],
        compiler_params=pltpu.CompilerParams(vmem_limit_bytes=8 << 20),
    )(*(pltpu.with_memory_space_constraint(x, pltpu.MemorySpace.VMEM) for x in outs))
    return disp_out.reshape(3, GRAINS, POINTS).transpose(1, 0, 2), stress, grid


def solution(mesh):
    both = ("slab", "helper")
    return jax.shard_map(
        per_device,
        mesh=mesh,
        in_specs=(
            P(None, None, both),
            P(None, both),
            P(both),
            P(both, None),
            P(None, None, both),
            P(),
            P(None, both),
            P(None, None, both),
        ),
        out_specs=(P(None, None, both), P(None, both), P(None, "slab", "helper")),
        check_vma=False,
    )
```

```python
import itertools
import random

import jax
import jax.numpy as jnp
from jax import lax
from jax.experimental import pallas as pl
from jax.experimental.pallas import tpu as pltpu
from jax.sharding import PartitionSpec as P

MESH = pl.DeviceIdType.MESH
GRAINS = 400
FLAT = 1200
POINTS = 128
WIDE = 3 * POINTS
SLOTS = 256
HELPERS = 8
SLABS = 16
DEVICES = 128
HEAD = 256
REST = GRAINS - HEAD
TAIL = REST - 128
FIRST = 12
SECOND = 7
CORNERS = 8
BABY = 4
GIANT = 3
F32 = jnp.float32
BF16 = jnp.bfloat16


def halves(x):
    hi = x.astype(BF16)
    lo = (x - hi.astype(F32)).astype(BF16)
    return hi, lo


def dot(a, b):
    return jnp.dot(a, b, preferred_element_type=F32)


def dot2(a, b):
    width = b[0].shape[1]
    both = dot(a, jnp.concatenate(b, axis=1))
    return both[:, :width] + both[:, width:]


def dot_exact(a, x):
    hi = x.astype(BF16)
    mid, lo = halves(x - hi.astype(F32))
    width = x.shape[1]
    both = dot(a, jnp.concatenate([hi, mid, lo], axis=1))
    return both[:, :width] + (both[:, width : 2 * width] + both[:, 2 * width :])


def dot3(a, b):
    return dot2(a[0], b) + dot(a[1], b[0])


def dot_nt(a, b):
    return lax.dot_general(a, b, (((1,), (1,)), ((), ())), preferred_element_type=F32)


def ring(a):
    return min(a, 4 - a)


def hops(offset):
    return ring(offset[0]) + ring(offset[1]) + ring(offset[2])


SHUFFLED = [
    offset for offset in itertools.product(range(4), range(4), range(4), range(2)) if any(offset)
]
random.Random(1).shuffle(SHUFFLED)
FARTHEST = sorted(SHUFFLED, key=lambda offset: -hops(offset))


def in_plane(offset):
    return 0 in offset[:3]


NEAR = [offset for offset in FARTHEST if in_plane(offset)]
ORDERS = (sorted(SHUFFLED, key=lambda offset: not in_plane(offset)), FARTHEST)


def kernel(
    cached_hbm, disp_hbm, mask_hbm, strain_hbm, counts_hbm, assign_hbm, node_hbm, grads_hbm,
    disp_out, stress_ref, grid_ref,
    cached, disp, mask, strain, counts_ref, assign, node, grads,
    turned, sent_first, sent_second, got_first, got_second, part, pulled, pos, met,
    sums_hi, sums_lo, leaps_hi, leaps_lo, first_hi, first_lo, second_hi, second_lo, contact, hit, spread,
    grid_out, own_got, low_got, high_got,
    load_sem, line_sem, send_sem, recv_sem, own_sem, grid_own_sem, grid_send, grid_recv,
):
    slab = lax.axis_index("slab")
    helper = lax.axis_index("helper")
    me = slab * HELPERS + helper

    moves = [(cached_hbm, cached)]
    for d in range(3):
        moves.append(
            (disp_hbm.at[pl.ds(d * GRAINS, GRAINS)], disp.at[:, pl.ds(d * POINTS, POINTS)])
        )
    moves += [
        (mask_hbm, mask), (strain_hbm, strain), (counts_hbm, counts_ref),
        (assign_hbm, assign), (node_hbm, node), (grads_hbm, grads),
    ]
    loads = [
        pltpu.make_async_copy(source, target, load_sem.at[i])
        for i, (source, target) in enumerate(moves)
    ]
    for copy in loads:
        copy.start()

    z, x, y, core = slab // 4, lax.rem(slab, 4), helper // 2, lax.rem(helper, 2)
    slab_at = {
        (a, b): lax.rem(z + a, 4) * 4 + lax.rem(x + b, 4) for a in range(4) for b in range(4)
    }
    helper_at = {
        (a, b): lax.rem(y + a, 4) * 2 + lax.rem(core + b, 2) for a in range(4) for b in range(2)
    }

    def at(offset):
        return slab_at[offset[:2]], helper_at[offset[2:]]

    barrier = pltpu.get_barrier_semaphore()
    for offset in NEAR:
        pl.semaphore_signal(barrier, inc=1, device_id=at(offset), device_id_type=MESH)

    @pl.when(slab == 0)
    def _():
        low_got[...] = jnp.zeros_like(low_got)

    @pl.when(slab == SLABS - 1)
    def _():
        high_got[...] = jnp.zeros_like(high_got)

    loads[0].wait()
    def slot(c):
        return pl.ds(c, DEVICES, stride=2)

    for e in range(3):
        for j in range(2):
            turned[2 * e + j] = cached[pl.ds(e * GRAINS + 128 * j, 128), :].T
            for c in range(2):
                sent_first[pl.ds(6 * c + 2 * e + j, DEVICES, stride=FIRST), :] = turned[
                    2 * e + j, slot(c), :
                ]

    def fill_second():
        for e in range(3):
            turned[6 + e] = cached[pl.ds(e * GRAINS + HEAD, 128), :].T
            for c in range(2):
                sent_second[pl.ds(3 * c + e, DEVICES, stride=SECOND), :] = turned[6 + e, slot(c), :]
        tail = [cached[pl.ds(e * GRAINS + GRAINS - TAIL, TAIL), :] for e in range(3)]
        turned[9] = jnp.concatenate(
            tail + tail + [jnp.zeros((128 - 6 * TAIL, SLOTS), F32)], axis=0
        ).T
        lane = lax.broadcasted_iota(jnp.int32, (DEVICES, 128), 1)
        sent_second[pl.ds(6, DEVICES, stride=SECOND), :] = jnp.where(
            lane < 3 * TAIL, turned[9, slot(0), :], turned[9, slot(1), :]
        )

    pl.semaphore_wait(barrier, len(NEAR))
    for a in (2, 1, 3):
        pl.semaphore_signal(line_sem, inc=1, device_id=at((a, 0, 0, 0)), device_id_type=MESH)

    waves = ((sent_first, got_first, FIRST), (sent_second, got_second, SECOND))
    for wave, (sent, got, rows) in enumerate(waves):
        if wave == 1:
            fill_second()
        for i, offset in enumerate(ORDERS[wave]):
            if wave == 0 and i == len(NEAR):
                pl.semaphore_wait(line_sem, 3)
            to_slab, to_helper = at(offset)
            pltpu.make_async_remote_copy(
                src_ref=sent.at[pl.ds((to_slab * HELPERS + to_helper) * rows, rows)],
                dst_ref=got.at[pl.ds(me * rows, rows)],
                send_sem=send_sem.at[wave],
                recv_sem=recv_sem.at[wave],
                device_id=(to_slab, to_helper),
                device_id_type=MESH,
            ).start()
    own = [
        pltpu.make_async_copy(
            sent.at[pl.ds(me * rows, rows)], got.at[pl.ds(me * rows, rows)], own_sem.at[wave]
        )
        for wave, (sent, got, rows) in enumerate(waves)
    ]
    for copy in own:
        copy.start()

    for copy in loads[1:]:
        copy.wait()
    stiff = mask[...].astype(F32)
    scale = jnp.sum(stiff, axis=1, keepdims=True) + 1.0
    rate = 0.8 / scale
    contact[...] = stiff.astype(BF16)

    def prepare():
        rate_row = 0.8 / (jnp.sum(mask[...].astype(F32), axis=0, keepdims=True) + 1.0)
        g_at = lax.broadcasted_iota(jnp.int32, (GRAINS, GRAINS), 0)
        h_at = lax.broadcasted_iota(jnp.int32, (GRAINS, GRAINS), 1)
        once = jnp.where(g_at == h_at, 0.2, 0.0) + rate * mask[...].astype(F32)

        def put(i, power):
            hi, lo = halves(power)
            side, at = i // GIANT, i % GIANT
            first_hi[side, :, pl.ds(at * HEAD, HEAD)] = hi[:, :HEAD]
            first_lo[side, :, pl.ds(at * HEAD, HEAD)] = lo[:, :HEAD]
            second_hi[side, :, pl.ds(at * REST, REST)] = hi[:, HEAD:]
            second_lo[side, :, pl.ds(at * REST, REST)] = lo[:, HEAD:]
            return hi, lo

        def put_turned(i, power):
            put(i, power * (1.25 * scale) * rate_row)

        def put_sum(i, value):
            sums_hi[i], sums_lo[i] = halves(value)

        put_turned(0, once)
        once_h = halves(once)
        summed = (jnp.where(g_at == h_at, 1.0, 0.0) + once) * rate_row
        put_sum(0, summed)
        twice = dot3(once_h, once_h)
        put_turned(1, twice)
        summed = summed + twice * rate_row
        put_sum(1, summed)
        twice_h = halves(twice)
        thrice = dot3(twice_h, once_h)
        put_turned(2, thrice)
        put_sum(2, summed + thrice * rate_row)
        fourth_h = put(3, dot3(twice_h, twice_h))
        leaps_hi[0], leaps_lo[0] = fourth_h
        eighth_h = put(4, dot3(fourth_h, fourth_h))
        leaps_hi[1], leaps_lo[1] = eighth_h
        put(5, dot3(eighth_h, fourth_h))

    prepare()

    def summed(i, x_h):
        return dot3((sums_hi[i], sums_lo[i]), x_h)

    def leap(i, x):
        return dot3((leaps_hi[i], leaps_lo[i]), halves(x))

    counts = jnp.concatenate([counts_ref[...]] * 3, axis=1)
    start = disp[...]
    remainder, quarter = lax.rem(counts, BABY), counts // BABY

    sides = (remainder, quarter)

    def masked(index, x_h):
        keeps = [jnp.where(index == i + 1, 1.0, 0.0).astype(BF16) for i in range(GIANT)]
        return [jnp.concatenate([x * keep for keep in keeps], axis=0) for x in x_h]

    def first_part(side, x_h):
        return dot3((first_hi[side], first_lo[side]), masked(sides[side], x_h))

    def second_part(side, x_h):
        return dot3((second_hi[side], second_lo[side]), masked(sides[side], x_h))

    def whole(side, x):
        return first_part(side, halves(x[:HEAD])) + second_part(side, halves(x[HEAD:]))

    free = jnp.where(remainder == 0, start, rate * whole(0, start * (1.25 * scale)))
    free = jnp.where(quarter == 0, free, whole(1, free))
    part[...] = free
    pulled[...] = scale * free - dot_exact(contact[...], free)

    a_row = jnp.broadcast_to(assign[...], (POINTS, POINTS))
    a_col = a_row.T
    p_at = lax.broadcasted_iota(jnp.int32, (POINTS, POINTS), 0)
    q_at = lax.broadcasted_iota(jnp.int32, (POINTS, POINTS), 1)
    rank = jnp.sum(
        jnp.where((a_row == a_col) & (q_at < p_at), 1.0, 0.0), axis=1, keepdims=True
    ).astype(jnp.int32)
    column = rank * DEVICES + a_col
    column = jnp.concatenate([column, column], axis=1)
    slot_at = lax.broadcasted_iota(jnp.int32, (POINTS, SLOTS), 1)
    pick = jnp.where(column == slot_at, 1.0, 0.0).astype(BF16)

    for k in range(CORNERS):
        value = node[pl.ds(k, 1), :]
        layer = value // 1024
        target = lax.rem(value, 1024) // 128
        low = lax.rem(value, 128)
        lanes = pl.ds(k * POINTS, POINTS)
        spread[:, lanes] = jnp.where(p_at == low, 1.0, 0.0).astype(BF16)
        hit[:, lanes] = jnp.where(p_at // 4 == target * 4 + layer, 1.0, 0.0)

    def chosen(slots, x):
        hi, lo = halves(x)
        return (dot(slots, hi) + dot(slots, lo)).T

    def arrived(wave):
        own[wave].wait()
        sent, _, rows = waves[wave]
        everything = sent.at[pl.ds(0, (DEVICES - 1) * rows)]
        pltpu.make_async_copy(everything, everything, recv_sem.at[wave]).wait()

    arrived(0)
    for e in range(3):
        for j in range(2):
            both = [
                got_first[pl.ds(6 * c + 2 * e + j, DEVICES, stride=FIRST), :] for c in range(2)
            ]
            pos[pl.ds(128 * j, 128), pl.ds(e * POINTS, POINTS)] = chosen(
                pick, jnp.concatenate(both, axis=0)
            )
    place_h = halves(pos[pl.ds(0, HEAD), :])
    for side in range(2):
        met[side] = first_part(side, place_h)

    arrived(1)
    for e in range(3):
        both = [got_second[pl.ds(3 * c + e, DEVICES, stride=SECOND), :] for c in range(2)]
        pos[pl.ds(HEAD, 128), pl.ds(e * POINTS, POINTS)] = chosen(
            pick, jnp.concatenate(both, axis=0)
        )
    tails = got_second[pl.ds(6, DEVICES, stride=SECOND), :]
    tails = (
        chosen(pick[:, :DEVICES], tails)[: 3 * TAIL]
        + chosen(pick[:, DEVICES:], tails)[3 * TAIL : 6 * TAIL]
    )
    for e in range(3):
        pos[pl.ds(HEAD + 128, TAIL), pl.ds(e * POINTS, POINTS)] = tails[e * TAIL : (e + 1) * TAIL]
    place_h = halves(pos[pl.ds(HEAD, REST), :])
    place = pos[...]
    inner, outer = [
        jnp.where(index == 0, place, met[side]) + second_part(side, place_h)
        for side, index in enumerate(sides)
    ]

    def across(x, e):
        return x[:, e * POINTS : (e + 1) * POINTS]

    def over_grains(a, d, b, e):
        return jnp.sum(across(a, d) * across(b, e), axis=0, keepdims=True)

    overlap = [
        [over_grains(place, e, place, f) - over_grains(outer, e, inner, f) for f in range(3)]
        for e in range(3)
    ]
    moments = [
        [
            (
                over_grains(pulled[...], d, place, e)
                + sum(strain[pl.ds(3 * d + f, 1), :] * overlap[e][f] for f in range(3))
            )
            / GRAINS
            for e in range(3)
        ]
        for d in range(3)
    ]
    stress = [[0.5 * (moments[d][e] + moments[e][d]) for e in range(3)] for d in range(3)]
    for d in range(3):
        for e in range(3):
            stress_ref[pl.ds(3 * d + e, 1), :] = stress[d][e]

    nothing = jnp.zeros((1, POINTS), F32)
    rows = [
        jnp.concatenate([stress[0][d], stress[1][d], stress[2][d], nothing] * 2, axis=0)
        for d in range(3)
    ]
    contrib = jnp.concatenate(
        [-sum(rows[d] * grads[d, pl.ds(k, 1), :] for d in range(3)) for k in range(CORNERS)], axis=1
    )
    hi, lo = halves(jnp.concatenate([contrib] * 16, axis=0) * hit[...])
    grid_out[...] = dot_nt(hi, spread[...]) + dot_nt(lo, spread[...])
    def grid_copy(first_row, count, kind, buffer, to_slab, to_helper):
        return pltpu.make_async_remote_copy(
            src_ref=grid_out.at[pl.ds(to_helper * 16 + first_row, count)],
            dst_ref=buffer.at[helper],
            send_sem=grid_send.at[kind],
            recv_sem=grid_recv.at[kind],
            device_id=(to_slab, to_helper),
            device_id_type=MESH,
        )

    order = (4, 5, 3, 2, 6, 7, 1)

    @pl.when(slab > 0)
    def _():
        for ahead in order + (0,):
            grid_copy(0, 4, 1, high_got, slab - 1, lax.rem(helper + ahead, HELPERS)).start()

    for ahead in order:
        grid_copy(4, 8, 0, own_got, slab, lax.rem(helper + ahead, HELPERS)).start()

    @pl.when(slab < SLABS - 1)
    def _():
        for ahead in order + (0,):
            grid_copy(12, 4, 2, low_got, slab + 1, lax.rem(helper + ahead, HELPERS)).start()

    mine = pltpu.make_async_copy(
        grid_out.at[pl.ds(helper * 16 + 4, 8)], own_got.at[helper], grid_own_sem
    )
    mine.start()

    @pl.when(slab >= 0)
    def _():
        place = pos[...]
        place_h = halves(place)

        def only(index):
            keep = jnp.where(remainder == index, 1.0, 0.0).astype(BF16)
            return [x * keep for x in place_h]

        some = (
            jnp.where(remainder == 1, rate * place, 0.0) + summed(0, only(2)) + summed(1, only(3))
        )
        full = summed(2, place_h)

        def term(j):
            return jnp.where(quarter > j, full, jnp.where(quarter == j, some, 0.0))

        total = term(0) + leap(0, term(1)) + leap(1, term(2))
        for d in range(3):
            disp_out[pl.ds(d * GRAINS, GRAINS), :] = part[:, pl.ds(d * POINTS, POINTS)] + sum(
                strain[pl.ds(3 * d + e, 1), :] * across(total, e) for e in range(3)
            )

    mine.wait()

    @pl.when(slab < SLABS - 1)
    def _():
        pltpu.make_async_copy(high_got, high_got, grid_recv.at[1]).wait()

    @pl.when(slab > 0)
    def _():
        pltpu.make_async_copy(low_got, low_got, grid_recv.at[2]).wait()

    seven = own_got.at[pl.ds(0, HELPERS - 1)]
    pltpu.make_async_copy(seven, seven, grid_recv.at[0]).wait()
    here = jnp.sum(own_got[...], axis=0)
    from_below, from_above = jnp.sum(low_got[...], axis=0), jnp.sum(high_got[...], axis=0)
    here = here + jnp.concatenate([from_below, from_above], axis=0)
    for c in range(3):
        for layer in range(2):
            grid_ref[c, pl.ds(layer, 1), :] = here[4 * layer + c : 4 * layer + c + 1]

    for wave, (sent, _, rows) in enumerate(waves):
        everything = sent.at[pl.ds(0, (DEVICES - 1) * rows)]
        pltpu.make_async_copy(everything, everything, send_sem.at[wave]).wait()

    @pl.when(slab > 0)
    def _():
        pltpu.make_async_copy(high_got, high_got, grid_send.at[1]).wait()

    @pl.when(slab < SLABS - 1)
    def _():
        pltpu.make_async_copy(low_got, low_got, grid_send.at[2]).wait()

    pltpu.make_async_copy(seven, seven, grid_send.at[0]).wait()


PIECES = 6


def hand_over(disp_in, stress_in, grid_in, disp_out, stress_out, grid_out, sems):
    rows = FLAT // PIECES
    copies = [
        pltpu.make_async_copy(
            disp_in.at[pl.ds(i * rows, rows)], disp_out.at[pl.ds(i * rows, rows)], sems.at[i]
        )
        for i in range(PIECES)
    ]
    copies.append(pltpu.make_async_copy(stress_in, stress_out, sems.at[PIECES]))
    copies.append(pltpu.make_async_copy(grid_in, grid_out, sems.at[PIECES + 1]))
    for copy in copies:
        copy.start()
    for copy in copies:
        copy.wait()


def per_device(disp, strain, counts, assign, cached_pos, contact_mask, node_index, node_grads):
    vmem = pl.BlockSpec(memory_space=pltpu.VMEM)
    hbm = pl.BlockSpec(memory_space=pltpu.MemorySpace.HBM)
    shapes = ((FLAT, POINTS), (9, POINTS), (3, 2, 128))

    def keep(x):
        return pltpu.with_memory_space_constraint(x, pltpu.MemorySpace.HBM)

    outs = pl.pallas_call(
        kernel,
        out_shape=tuple(pltpu.VMEM(shape, F32) for shape in shapes),
        in_specs=[hbm] * 8,
        out_specs=(vmem,) * 3,
        scratch_shapes=[
            pltpu.VMEM((FLAT, SLOTS), F32),
            pltpu.VMEM((GRAINS, WIDE), F32),
            pltpu.VMEM((GRAINS, GRAINS), jnp.int32),
            pltpu.VMEM((9, POINTS), F32),
            pltpu.VMEM((1, POINTS), jnp.int32),
            pltpu.VMEM((1, POINTS), jnp.int32),
            pltpu.VMEM((CORNERS, POINTS), jnp.int32),
            pltpu.VMEM((3, CORNERS, POINTS), F32),
            pltpu.VMEM((10, SLOTS, 128), F32),
            pltpu.VMEM((DEVICES * FIRST, 128), F32),
            pltpu.VMEM((DEVICES * SECOND, 128), F32),
            pltpu.VMEM((DEVICES * FIRST, 128), F32),
            pltpu.VMEM((DEVICES * SECOND, 128), F32),
            pltpu.VMEM((GRAINS, WIDE), F32),
            pltpu.VMEM((GRAINS, WIDE), F32),
            pltpu.VMEM((GRAINS, WIDE), F32),
            pltpu.VMEM((2, GRAINS, WIDE), F32),
            pltpu.VMEM((GIANT, GRAINS, GRAINS), BF16),
            pltpu.VMEM((GIANT, GRAINS, GRAINS), BF16),
            pltpu.VMEM((2, GRAINS, GRAINS), BF16),
            pltpu.VMEM((2, GRAINS, GRAINS), BF16),
            pltpu.VMEM((2, GRAINS, GIANT * HEAD), BF16),
            pltpu.VMEM((2, GRAINS, GIANT * HEAD), BF16),
            pltpu.VMEM((2, GRAINS, GIANT * REST), BF16),
            pltpu.VMEM((2, GRAINS, GIANT * REST), BF16),
            pltpu.VMEM((GRAINS, GRAINS), BF16),
            pltpu.VMEM((128, CORNERS * POINTS), F32),
            pltpu.VMEM((128, CORNERS * POINTS), BF16),
            pltpu.VMEM((128, 128), F32),
            pltpu.VMEM((HELPERS, 8, 128), F32),
            pltpu.VMEM((HELPERS, 4, 128), F32),
            pltpu.VMEM((HELPERS, 4, 128), F32),
            pltpu.SemaphoreType.DMA((10,)),
            pltpu.SemaphoreType.REGULAR,
            pltpu.SemaphoreType.DMA((2,)),
            pltpu.SemaphoreType.DMA((2,)),
            pltpu.SemaphoreType.DMA((2,)),
            pltpu.SemaphoreType.DMA,
            pltpu.SemaphoreType.DMA((3,)),
            pltpu.SemaphoreType.DMA((3,)),
        ],
        compiler_params=pltpu.CompilerParams(
            collective_id=0, has_side_effects=True, vmem_limit_bytes=56 << 20
        ),
    )(
        keep(cached_pos.transpose(1, 0, 2).reshape(FLAT, SLOTS)),
        keep(disp.transpose(1, 0, 2).reshape(FLAT, POINTS)),
        keep(contact_mask),
        keep(strain),
        keep(counts.reshape(1, POINTS)),
        keep(assign.reshape(1, POINTS)),
        keep(node_index),
        keep(node_grads),
    )
    disp_out, stress, grid = pl.pallas_call(
        hand_over,
        out_shape=tuple(jax.ShapeDtypeStruct(shape, F32) for shape in shapes),
        in_specs=[vmem] * 3,
        out_specs=(hbm,) * 3,
        scratch_shapes=[pltpu.SemaphoreType.DMA((PIECES + 2,))],
        compiler_params=pltpu.CompilerParams(vmem_limit_bytes=8 << 20),
    )(*(pltpu.with_memory_space_constraint(x, pltpu.MemorySpace.VMEM) for x in outs))
    return disp_out.reshape(3, GRAINS, POINTS).transpose(1, 0, 2), stress, grid


def solution(mesh):
    both = ("slab", "helper")
    return jax.shard_map(
        per_device,
        mesh=mesh,
        in_specs=(
            P(None, None, both),
            P(None, both),
            P(both),
            P(both, None),
            P(None, None, both),
            P(),
            P(None, both),
            P(None, None, both),
        ),
        out_specs=(P(None, None, both), P(None, both), P(None, "slab", "helper")),
        check_vma=False,
    )
```

```python
import itertools
import random

import jax
import jax.numpy as jnp
from jax import lax
from jax.experimental import pallas as pl
from jax.experimental.pallas import tpu as pltpu
from jax.sharding import PartitionSpec as P

MESH = pl.DeviceIdType.MESH
GRAINS = 400
FLAT = 1200
POINTS = 128
WIDE = 3 * POINTS
SLOTS = 256
HELPERS = 8
SLABS = 16
DEVICES = 128
HEAD = 256
REST = GRAINS - HEAD
TAIL = REST - 128
FIRST = 12
SECOND = 7
CORNERS = 8
BABY = 4
GIANT = 3
F32 = jnp.float32
BF16 = jnp.bfloat16


def halves(x):
    hi = x.astype(BF16)
    lo = (x - hi.astype(F32)).astype(BF16)
    return hi, lo


def dot(a, b):
    return jnp.dot(a, b, preferred_element_type=F32)


def dot2(a, b):
    width = b[0].shape[1]
    both = dot(a, jnp.concatenate(b, axis=1))
    return both[:, :width] + both[:, width:]


def dot3(a, b):
    return dot2(a[0], b) + dot(a[1], b[0])


def dot_nt(a, b):
    return lax.dot_general(a, b, (((1,), (1,)), ((), ())), preferred_element_type=F32)


def ring(a):
    return min(a, 4 - a)


def hops(offset):
    return ring(offset[0]) + ring(offset[1]) + ring(offset[2])


SHUFFLED = [
    offset for offset in itertools.product(range(4), range(4), range(4), range(2)) if any(offset)
]
random.Random(1).shuffle(SHUFFLED)
FARTHEST = sorted(SHUFFLED, key=lambda offset: -hops(offset))


def in_plane(offset):
    return 0 in offset[:3]


NEAR = [offset for offset in FARTHEST if in_plane(offset)]
ORDERS = (sorted(FARTHEST, key=lambda offset: not in_plane(offset)), FARTHEST)


def kernel(
    cached_hbm, disp_hbm, mask_hbm, strain_hbm, counts_hbm, assign_hbm, node_hbm, grads_hbm,
    disp_out, stress_ref, grid_ref,
    cached, disp, mask, strain, counts_ref, assign, node, grads,
    turned, sent_first, sent_second, got_first, got_second, part, pulled, pos, met,
    steps_hi, steps_lo, first_hi, first_lo, second_hi, second_lo, contact, hit, spread,
    grid_out, own_got, low_got, high_got,
    load_sem, line_sem, send_sem, recv_sem, own_sem, grid_own_sem, grid_send, grid_recv,
):
    slab = lax.axis_index("slab")
    helper = lax.axis_index("helper")
    me = slab * HELPERS + helper

    moves = [(cached_hbm, cached)]
    for d in range(3):
        moves.append(
            (disp_hbm.at[pl.ds(d * GRAINS, GRAINS)], disp.at[:, pl.ds(d * POINTS, POINTS)])
        )
    moves += [
        (mask_hbm, mask), (strain_hbm, strain), (counts_hbm, counts_ref),
        (assign_hbm, assign), (node_hbm, node), (grads_hbm, grads),
    ]
    loads = [
        pltpu.make_async_copy(source, target, load_sem.at[i])
        for i, (source, target) in enumerate(moves)
    ]
    for copy in loads:
        copy.start()

    z, x, y, core = slab // 4, lax.rem(slab, 4), helper // 2, lax.rem(helper, 2)
    slab_at = {
        (a, b): lax.rem(z + a, 4) * 4 + lax.rem(x + b, 4) for a in range(4) for b in range(4)
    }
    helper_at = {
        (a, b): lax.rem(y + a, 4) * 2 + lax.rem(core + b, 2) for a in range(4) for b in range(2)
    }

    def at(offset):
        return slab_at[offset[:2]], helper_at[offset[2:]]

    barrier = pltpu.get_barrier_semaphore()
    for offset in NEAR:
        pl.semaphore_signal(barrier, inc=1, device_id=at(offset), device_id_type=MESH)

    @pl.when(slab == 0)
    def _():
        low_got[...] = jnp.zeros_like(low_got)

    @pl.when(slab == SLABS - 1)
    def _():
        high_got[...] = jnp.zeros_like(high_got)

    loads[0].wait()
    for e in range(3):
        for j in range(3):
            turned[3 * e + j] = cached[pl.ds(e * GRAINS + 128 * j, 128), :].T
    tail = [cached[pl.ds(e * GRAINS + GRAINS - TAIL, TAIL), :] for e in range(3)]
    turned[9] = jnp.concatenate(
        tail + tail + [jnp.zeros((128 - 6 * TAIL, SLOTS), F32)], axis=0
    ).T
    for c in range(2):
        mine = pl.ds(c, DEVICES, stride=2)
        for e in range(3):
            for j in range(2):
                sent_first[pl.ds(6 * c + 2 * e + j, DEVICES, stride=FIRST), :] = turned[
                    3 * e + j, mine, :
                ]
            sent_second[pl.ds(3 * c + e, DEVICES, stride=SECOND), :] = turned[3 * e + 2, mine, :]
    lane = lax.broadcasted_iota(jnp.int32, (DEVICES, 128), 1)
    sent_second[pl.ds(6, DEVICES, stride=SECOND), :] = jnp.where(
        lane < 3 * TAIL,
        turned[9, pl.ds(0, DEVICES, stride=2), :],
        turned[9, pl.ds(1, DEVICES, stride=2), :],
    )

    for copy in loads[1:]:
        copy.wait()
    stiff = mask[...].astype(F32)
    scale = jnp.sum(stiff, axis=1, keepdims=True) + 1.0
    rate = 0.8 / scale
    contact[...] = stiff.astype(BF16)

    def prepare():
        rate_row = 0.8 / (jnp.sum(mask[...].astype(F32), axis=0, keepdims=True) + 1.0)
        g_at = lax.broadcasted_iota(jnp.int32, (GRAINS, GRAINS), 0)
        h_at = lax.broadcasted_iota(jnp.int32, (GRAINS, GRAINS), 1)
        once = jnp.where(g_at == h_at, 0.2, 0.0) + rate * mask[...].astype(F32)

        def put(i, power):
            hi, lo = halves(power)
            steps_hi[pl.ds(i * GRAINS, GRAINS), :] = hi
            steps_lo[pl.ds(i * GRAINS, GRAINS), :] = lo
            side, at = i // GIANT, i % GIANT
            first_hi[side, :, pl.ds(at * HEAD, HEAD)] = hi[:, :HEAD]
            first_lo[side, :, pl.ds(at * HEAD, HEAD)] = lo[:, :HEAD]
            second_hi[side, :, pl.ds(at * REST, REST)] = hi[:, HEAD:]
            second_lo[side, :, pl.ds(at * REST, REST)] = lo[:, HEAD:]
            return hi, lo

        def put_turned(i, power):
            put(i, power * (1.25 * scale) * rate_row)

        put_turned(0, once)
        once_h = halves(once)
        twice = dot3(once_h, once_h)
        put_turned(1, twice)
        twice_h = halves(twice)
        put_turned(2, dot3(twice_h, once_h))
        fourth_h = put(3, dot3(twice_h, twice_h))
        eighth_h = put(4, dot3(fourth_h, fourth_h))
        put(5, dot3(eighth_h, fourth_h))

    pl.semaphore_wait(barrier, len(NEAR))
    for a in (2, 1, 3):
        pl.semaphore_signal(line_sem, inc=1, device_id=at((a, 0, 0, 0)), device_id_type=MESH)

    waves = ((sent_first, got_first, FIRST), (sent_second, got_second, SECOND))
    for wave, (sent, got, rows) in enumerate(waves):
        for i, offset in enumerate(ORDERS[wave]):
            if wave == 0 and i == len(NEAR):
                pl.semaphore_wait(line_sem, 3)
            to_slab, to_helper = at(offset)
            pltpu.make_async_remote_copy(
                src_ref=sent.at[pl.ds((to_slab * HELPERS + to_helper) * rows, rows)],
                dst_ref=got.at[pl.ds(me * rows, rows)],
                send_sem=send_sem.at[wave],
                recv_sem=recv_sem.at[wave],
                device_id=(to_slab, to_helper),
                device_id_type=MESH,
            ).start()
    own = [
        pltpu.make_async_copy(
            sent.at[pl.ds(me * rows, rows)], got.at[pl.ds(me * rows, rows)], own_sem.at[wave]
        )
        for wave, (sent, got, rows) in enumerate(waves)
    ]
    for copy in own:
        copy.start()

    prepare()

    def step(i):
        rows = pl.ds(i * GRAINS, GRAINS)
        return steps_hi[rows, :], steps_lo[rows, :]

    def leap(i, x):
        return dot3(step(BABY - 2 + i), halves(x))

    counts = jnp.concatenate([counts_ref[...]] * 3, axis=1)
    start = disp[...]
    remainder, quarter = lax.rem(counts, BABY), counts // BABY

    def by(index, choices):
        value = choices[-1]
        for i in reversed(range(len(choices) - 1)):
            value = jnp.where(index == i, choices[i], value)
        return value

    start_h = halves(start * (1.25 * scale))
    moved_start = by(remainder, [start] + [rate * dot3(step(i), start_h) for i in range(BABY - 1)])
    terms = [jnp.where(quarter == j, moved_start, 0.0) for j in range(GIANT + 1)]
    free = terms[0] + leap(1, terms[1]) + leap(2, terms[2]) + leap(3, terms[3])
    part[...] = free
    pulled[...] = scale * free - dot2(contact[...], halves(free))

    a_row = jnp.broadcast_to(assign[...], (POINTS, POINTS))
    a_col = a_row.T
    p_at = lax.broadcasted_iota(jnp.int32, (POINTS, POINTS), 0)
    q_at = lax.broadcasted_iota(jnp.int32, (POINTS, POINTS), 1)
    rank = jnp.sum(
        jnp.where((a_row == a_col) & (q_at < p_at), 1.0, 0.0), axis=1, keepdims=True
    ).astype(jnp.int32)
    column = rank * DEVICES + a_col
    column = jnp.concatenate([column, column], axis=1)
    slot_at = lax.broadcasted_iota(jnp.int32, (POINTS, SLOTS), 1)
    pick = jnp.where(column == slot_at, 1.0, 0.0).astype(BF16)

    for k in range(CORNERS):
        value = node[pl.ds(k, 1), :]
        layer = value // 1024
        target = lax.rem(value, 1024) // 128
        low = lax.rem(value, 128)
        lanes = pl.ds(k * POINTS, POINTS)
        spread[:, lanes] = jnp.where(p_at == low, 1.0, 0.0).astype(BF16)
        hit[:, lanes] = jnp.where(p_at // 4 == target * 4 + layer, 1.0, 0.0)

    def chosen(slots, x):
        hi, lo = halves(x)
        return (dot(slots, hi) + dot(slots, lo)).T

    def arrived(wave):
        own[wave].wait()
        sent, _, rows = waves[wave]
        everything = sent.at[pl.ds(0, (DEVICES - 1) * rows)]
        pltpu.make_async_copy(everything, everything, recv_sem.at[wave]).wait()

    def masked(index, x_h):
        keeps = [jnp.where(index == i + 1, 1.0, 0.0).astype(BF16) for i in range(GIANT)]
        return [jnp.concatenate([x * keep for keep in keeps], axis=0) for x in x_h]

    arrived(0)
    for e in range(3):
        for j in range(2):
            both = [
                got_first[pl.ds(6 * c + 2 * e + j, DEVICES, stride=FIRST), :] for c in range(2)
            ]
            pos[pl.ds(128 * j, 128), pl.ds(e * POINTS, POINTS)] = chosen(
                pick, jnp.concatenate(both, axis=0)
            )
    place_h = halves(pos[pl.ds(0, HEAD), :])
    sides = (remainder, quarter)
    for side, index in enumerate(sides):
        met[side] = dot3((first_hi[side], first_lo[side]), masked(index, place_h))

    arrived(1)
    for e in range(3):
        both = [got_second[pl.ds(3 * c + e, DEVICES, stride=SECOND), :] for c in range(2)]
        pos[pl.ds(HEAD, 128), pl.ds(e * POINTS, POINTS)] = chosen(
            pick, jnp.concatenate(both, axis=0)
        )
    tails = got_second[pl.ds(6, DEVICES, stride=SECOND), :]
    tails = (
        chosen(pick[:, :DEVICES], tails)[: 3 * TAIL]
        + chosen(pick[:, DEVICES:], tails)[3 * TAIL : 6 * TAIL]
    )
    for e in range(3):
        pos[pl.ds(HEAD + 128, TAIL), pl.ds(e * POINTS, POINTS)] = tails[e * TAIL : (e + 1) * TAIL]
    place_h = halves(pos[pl.ds(HEAD, REST), :])
    place = pos[...]
    inner, outer = [
        jnp.where(index == 0, place, met[side])
        + dot3((second_hi[side], second_lo[side]), masked(index, place_h))
        for side, index in enumerate(sides)
    ]

    def across(x, e):
        return x[:, e * POINTS : (e + 1) * POINTS]

    def over_grains(a, d, b, e):
        return jnp.sum(across(a, d) * across(b, e), axis=0, keepdims=True)

    overlap = [
        [over_grains(place, e, place, f) - over_grains(outer, e, inner, f) for f in range(3)]
        for e in range(3)
    ]
    moments = [
        [
            (
                over_grains(pulled[...], d, place, e)
                + sum(strain[pl.ds(3 * d + f, 1), :] * overlap[e][f] for f in range(3))
            )
            / GRAINS
            for e in range(3)
        ]
        for d in range(3)
    ]
    stress = [[0.5 * (moments[d][e] + moments[e][d]) for e in range(3)] for d in range(3)]
    for d in range(3):
        for e in range(3):
            stress_ref[pl.ds(3 * d + e, 1), :] = stress[d][e]

    nothing = jnp.zeros((1, POINTS), F32)
    rows = [
        jnp.concatenate([stress[0][d], stress[1][d], stress[2][d], nothing] * 2, axis=0)
        for d in range(3)
    ]
    contrib = jnp.concatenate(
        [-sum(rows[d] * grads[d, pl.ds(k, 1), :] for d in range(3)) for k in range(CORNERS)], axis=1
    )
    hi, lo = halves(jnp.concatenate([contrib] * 16, axis=0) * hit[...])
    grid_out[...] = dot_nt(hi, spread[...]) + dot_nt(lo, spread[...])
    def grid_copy(first_row, count, kind, buffer, to_slab, to_helper):
        return pltpu.make_async_remote_copy(
            src_ref=grid_out.at[pl.ds(to_helper * 16 + first_row, count)],
            dst_ref=buffer.at[helper],
            send_sem=grid_send.at[kind],
            recv_sem=grid_recv.at[kind],
            device_id=(to_slab, to_helper),
            device_id_type=MESH,
        )

    order = (4, 5, 3, 2, 6, 7, 1)

    @pl.when(slab > 0)
    def _():
        for ahead in order + (0,):
            grid_copy(0, 4, 1, high_got, slab - 1, lax.rem(helper + ahead, HELPERS)).start()

    for ahead in order:
        grid_copy(4, 8, 0, own_got, slab, lax.rem(helper + ahead, HELPERS)).start()

    @pl.when(slab < SLABS - 1)
    def _():
        for ahead in order + (0,):
            grid_copy(12, 4, 2, low_got, slab + 1, lax.rem(helper + ahead, HELPERS)).start()

    mine = pltpu.make_async_copy(
        grid_out.at[pl.ds(helper * 16 + 4, 8)], own_got.at[helper], grid_own_sem
    )
    mine.start()

    @pl.when(slab >= 0)
    def _():
        place = pos[...]
        place_h = halves(place)
        powers = [rate * place] + [rate * dot3(step(i), place_h) for i in range(BABY - 1)]
        terms = []
        for j in range(GIANT):
            term = jnp.zeros((GRAINS, WIDE), F32)
            for i in range(BABY):
                term = term + jnp.where(BABY * j + i < counts, powers[i], 0.0)
            terms.append(term)
        total = terms[0] + leap(1, terms[1]) + leap(2, terms[2])
        for d in range(3):
            disp_out[pl.ds(d * GRAINS, GRAINS), :] = part[:, pl.ds(d * POINTS, POINTS)] + sum(
                strain[pl.ds(3 * d + e, 1), :] * across(total, e) for e in range(3)
            )

    mine.wait()

    @pl.when(slab < SLABS - 1)
    def _():
        pltpu.make_async_copy(high_got, high_got, grid_recv.at[1]).wait()

    @pl.when(slab > 0)
    def _():
        pltpu.make_async_copy(low_got, low_got, grid_recv.at[2]).wait()

    seven = own_got.at[pl.ds(0, HELPERS - 1)]
    pltpu.make_async_copy(seven, seven, grid_recv.at[0]).wait()
    here = jnp.sum(own_got[...], axis=0)
    from_below, from_above = jnp.sum(low_got[...], axis=0), jnp.sum(high_got[...], axis=0)
    here = here + jnp.concatenate([from_below, from_above], axis=0)
    for c in range(3):
        for layer in range(2):
            grid_ref[c, pl.ds(layer, 1), :] = here[4 * layer + c : 4 * layer + c + 1]

    for wave, (sent, _, rows) in enumerate(waves):
        everything = sent.at[pl.ds(0, (DEVICES - 1) * rows)]
        pltpu.make_async_copy(everything, everything, send_sem.at[wave]).wait()

    @pl.when(slab > 0)
    def _():
        pltpu.make_async_copy(high_got, high_got, grid_send.at[1]).wait()

    @pl.when(slab < SLABS - 1)
    def _():
        pltpu.make_async_copy(low_got, low_got, grid_send.at[2]).wait()

    pltpu.make_async_copy(seven, seven, grid_send.at[0]).wait()


PIECES = 6


def hand_over(disp_in, stress_in, grid_in, disp_out, stress_out, grid_out, sems):
    rows = FLAT // PIECES
    copies = [
        pltpu.make_async_copy(
            disp_in.at[pl.ds(i * rows, rows)], disp_out.at[pl.ds(i * rows, rows)], sems.at[i]
        )
        for i in range(PIECES)
    ]
    copies.append(pltpu.make_async_copy(stress_in, stress_out, sems.at[PIECES]))
    copies.append(pltpu.make_async_copy(grid_in, grid_out, sems.at[PIECES + 1]))
    for copy in copies:
        copy.start()
    for copy in copies:
        copy.wait()


def per_device(disp, strain, counts, assign, cached_pos, contact_mask, node_index, node_grads):
    vmem = pl.BlockSpec(memory_space=pltpu.VMEM)
    hbm = pl.BlockSpec(memory_space=pltpu.MemorySpace.HBM)
    shapes = ((FLAT, POINTS), (9, POINTS), (3, 2, 128))

    def keep(x):
        return pltpu.with_memory_space_constraint(x, pltpu.MemorySpace.HBM)

    outs = pl.pallas_call(
        kernel,
        out_shape=tuple(pltpu.VMEM(shape, F32) for shape in shapes),
        in_specs=[hbm] * 8,
        out_specs=(vmem,) * 3,
        scratch_shapes=[
            pltpu.VMEM((FLAT, SLOTS), F32),
            pltpu.VMEM((GRAINS, WIDE), F32),
            pltpu.VMEM((GRAINS, GRAINS), jnp.int32),
            pltpu.VMEM((9, POINTS), F32),
            pltpu.VMEM((1, POINTS), jnp.int32),
            pltpu.VMEM((1, POINTS), jnp.int32),
            pltpu.VMEM((CORNERS, POINTS), jnp.int32),
            pltpu.VMEM((3, CORNERS, POINTS), F32),
            pltpu.VMEM((10, SLOTS, 128), F32),
            pltpu.VMEM((DEVICES * FIRST, 128), F32),
            pltpu.VMEM((DEVICES * SECOND, 128), F32),
            pltpu.VMEM((DEVICES * FIRST, 128), F32),
            pltpu.VMEM((DEVICES * SECOND, 128), F32),
            pltpu.VMEM((GRAINS, WIDE), F32),
            pltpu.VMEM((GRAINS, WIDE), F32),
            pltpu.VMEM((GRAINS, WIDE), F32),
            pltpu.VMEM((2, GRAINS, WIDE), F32),
            pltpu.VMEM((6 * GRAINS, GRAINS), BF16),
            pltpu.VMEM((6 * GRAINS, GRAINS), BF16),
            pltpu.VMEM((2, GRAINS, GIANT * HEAD), BF16),
            pltpu.VMEM((2, GRAINS, GIANT * HEAD), BF16),
            pltpu.VMEM((2, GRAINS, GIANT * REST), BF16),
            pltpu.VMEM((2, GRAINS, GIANT * REST), BF16),
            pltpu.VMEM((GRAINS, GRAINS), BF16),
            pltpu.VMEM((128, CORNERS * POINTS), F32),
            pltpu.VMEM((128, CORNERS * POINTS), BF16),
            pltpu.VMEM((128, 128), F32),
            pltpu.VMEM((HELPERS, 8, 128), F32),
            pltpu.VMEM((HELPERS, 4, 128), F32),
            pltpu.VMEM((HELPERS, 4, 128), F32),
            pltpu.SemaphoreType.DMA((10,)),
            pltpu.SemaphoreType.REGULAR,
            pltpu.SemaphoreType.DMA((2,)),
            pltpu.SemaphoreType.DMA((2,)),
            pltpu.SemaphoreType.DMA((2,)),
            pltpu.SemaphoreType.DMA,
            pltpu.SemaphoreType.DMA((3,)),
            pltpu.SemaphoreType.DMA((3,)),
        ],
        compiler_params=pltpu.CompilerParams(
            collective_id=0, has_side_effects=True, vmem_limit_bytes=56 << 20
        ),
    )(
        keep(cached_pos.transpose(1, 0, 2).reshape(FLAT, SLOTS)),
        keep(disp.transpose(1, 0, 2).reshape(FLAT, POINTS)),
        keep(contact_mask),
        keep(strain),
        keep(counts.reshape(1, POINTS)),
        keep(assign.reshape(1, POINTS)),
        keep(node_index),
        keep(node_grads),
    )
    disp_out, stress, grid = pl.pallas_call(
        hand_over,
        out_shape=tuple(jax.ShapeDtypeStruct(shape, F32) for shape in shapes),
        in_specs=[vmem] * 3,
        out_specs=(hbm,) * 3,
        scratch_shapes=[pltpu.SemaphoreType.DMA((PIECES + 2,))],
        compiler_params=pltpu.CompilerParams(vmem_limit_bytes=8 << 20),
    )(*(pltpu.with_memory_space_constraint(x, pltpu.MemorySpace.VMEM) for x in outs))
    return disp_out.reshape(3, GRAINS, POINTS).transpose(1, 0, 2), stress, grid


def solution(mesh):
    both = ("slab", "helper")
    return jax.shard_map(
        per_device,
        mesh=mesh,
        in_specs=(
            P(None, None, both),
            P(None, both),
            P(both),
            P(both, None),
            P(None, None, both),
            P(),
            P(None, both),
            P(None, None, both),
        ),
        out_specs=(P(None, None, both), P(None, both), P(None, "slab", "helper")),
        check_vma=False,
    )
```
